512 devices in a mesh: ep: 64 (over y, z_hi, x), tp: 8 (over z_lo, core).
Axes of the slice: x: 4, y: 8, z: 8 (z_hi: 2, z_lo: 4; z = z_hi * 4 + z_lo), core: 2. Of those that a mesh axis runs over, the one named last changes fastest.
Arguments:
- tokens: bfloat16 [65536, 1024], P(('ep', 'tp')), may hold values from -6 to 6
- gates: float32 [65536, 8], P(('ep', 'tp')), may hold values from 0.1 to 0.5
- routes: int32 [65536, 8], P(('ep', 'tp')), may hold values from 0 to 63, all different within a row; in each aligned block of 128 rows (0 to 127, 128 to 255, ...) at most 16 rows name the same one
- cotangent: bfloat16 [65536, 1024], P(('ep', 'tp')), may hold values from -6 to 6
- old_home: int32 [64], replicated, may hold values from 0 to 63, each once
- swap_flags: int32 [32], replicated, may hold values 0 or 1
- weights: bfloat16 [64, 3, 384, 1024], P('ep', None, 'tp'), may hold values from -0.3125 to 0.3125
- first_moment: float32 [64, 3, 384, 1024], P('ep', None, 'tp'), may hold values from -18 to 18
- second_moment: float32 [64, 3, 384, 1024], P('ep', None, 'tp'), may hold values from 1 to 1000
Outputs:
- layer_output_rows: bfloat16 [65536, 1024], P(('ep', 'tp'))
- token_gradient_rows: bfloat16 [65536, 1024], P(('ep', 'tp'))
- new_weights: bfloat16 [64, 3, 384, 1024], P('ep', None, 'tp')
- new_first: float32 [64, 3, 384, 1024], P('ep', None, 'tp')
- new_second: float32 [64, 3, 384, 1024], P('ep', None, 'tp')
The draws below stay inside these ranges and needn't reach their ends.
Inputs may be any that keep to these rules, and one draw needn't show every extreme that they name: `routes`: in the 128 rows of one device every expert is named exactly 16 times; each row names 8 different experts. `old_home`: each expert appears once.
All inputs are finite; a program needn't handle non-finite values.
Results may differ from the reference program's by a relative error of at most 0.025.
Values may be sent and summed in bfloat16 or wider, within the bound.
No kernel may reach another device: no remote copies, remote signals or barrier semaphores. Data moves between devices by JAX's collectives and lax.ppermute only.
A program may use at most 64 MiB of HBM per device.

```python
import math
import jax
import jax.numpy as jnp
import numpy as np
from jax import lax

D = 1024
FF = 384
TOP = 8
TOK_DEV = 128
EXPERTS = 64
PAIRS = 32
CAP = 16
TOKENS = 65536
N_EP = 64
N_TP = 8


def plant(result, rng, smallest, largest):
    shape = result.shape
    spot = [jax.random.randint(jax.random.fold_in(rng, axis), (), 0, shape[axis]) for axis in range(len(shape))]
    result = result.at[tuple(spot)].set(smallest)
    longest = shape.index(max(shape))
    spot[longest] = (spot[longest] + 1) % shape[longest]
    return result.at[tuple(spot)].set(largest)


def level_of(stream_key, dims, pieces, low, largest):
    def one(position, shards_of):
        draws = jax.random.uniform(jax.random.fold_in(jax.random.fold_in(stream_key, 6), position), (shards_of,), jnp.float32, low / len(pieces), largest / len(pieces))
        return jnp.repeat(jnp.exp(draws), dims[position] // shards_of).reshape((-1,) + (1,) * (len(dims) - position - 1))

    level = one(*pieces[0])
    for cut in pieces[1:]:
        level = level * one(*cut)
    return level


def assign_block(stream_key, own, number, rows, amount, top, bound, skew):
    ranking = jax.random.permutation(stream_key, amount)
    crowded, ordinary = load_shares(amount, rows * top, bound, skew, True), load_shares(amount, rows * top, bound, skew, False)
    places = jnp.arange(amount)

    def named(lengths, turn):
        used = int((lengths > 0).sum())
        fixed = max(1, used // 4)
        moved = fixed + (places - fixed + turn * (used - fixed)) % max(1, amount - fixed)
        return jnp.zeros((amount,), jnp.int32).at[ranking[jnp.where(places < fixed, places, moved)]].set(jnp.asarray(lengths, jnp.int32))

    lengths = jnp.where(number % 4 == 0, named(crowded, number // 4), named(ordinary, number - number // 4 - 1))
    mixed = jax.random.permutation(jax.random.fold_in(own, 3), amount)
    source_of, receiver = mixed[0:amount // 2 * 2:2], mixed[1:amount // 2 * 2:2]
    margin = jnp.minimum(lengths[source_of] - 1, bound - lengths[receiver]) // 2
    margin = jnp.where((source_of == ranking[0]) | (receiver == ranking[0]) | (lengths[receiver] == 0), 0, jnp.maximum(margin, 0))
    moved = jax.random.randint(jax.random.fold_in(own, 4), (amount // 2,), 0, 1 << 20) % (margin + 1)
    lengths = lengths.at[source_of].add(-moved).at[receiver].add(moved)
    labels = jnp.searchsorted(jnp.cumsum(lengths), jnp.arange(rows * top), side="right").astype(jnp.int32)
    listing = labels.reshape(top, rows).T
    listing = listing[jax.random.permutation(jax.random.fold_in(own, 1), rows)]
    turn = jax.random.randint(jax.random.fold_in(own, 2), (rows, 1), 0, top)
    return jnp.take_along_axis(listing, (jnp.arange(top)[None, :] + turn) % top, axis=1)


def load_shares(number_of, total, reach, slope, full):
    loads = [(1 << 20) // math.isqrt(standing ** slope) + 1 for standing in range(1, number_of + 1)]
    largest = reach if full else min(reach, max(-(-total // number_of), total * loads[0] // sum(loads)))
    least = 1 if total - largest >= number_of - 1 else 0
    given, surplus = [largest] + [least] * (number_of - 1), total - largest - least * (number_of - 1)
    while surplus > 0:
        movable = [i for i in range(1, number_of) if given[i] < largest] or [i for i in range(1, number_of) if given[i] < reach]
        pool, remaining = sum([loads[i] for i in movable]), surplus
        for i in movable:
            extra = min(reach - given[i], max(1, remaining * loads[i] // pool), surplus)
            given[i] = given[i] + extra
            surplus = surplus - extra
    return np.array(given)


def gaussian(stream_key, extent, width, limit, cuts=(), kind=jnp.bfloat16):
    drawn = width * jax.random.normal(stream_key, extent, jnp.float32)
    if cuts:
        drawn = drawn * level_of(stream_key, extent, cuts, -0.22, 0.18)
    return jnp.clip(drawn, -limit, limit).astype(kind)


def setup_inputs(seed: int = 0) -> dict:
    key_list = jax.random.split(jax.random.key(seed), 10)
    tokens = gaussian(key_list[0], (TOKENS, D), 1.0, 6.0, ((0, 512),))
    gates = jnp.clip(0.1 + 0.4 * jax.random.uniform(key_list[1], (TOKENS, TOP), jnp.float32) ** level_of(key_list[1], (TOKENS, TOP), ((0, 512),), -0.2, 0.2), 0.1, 0.5)
    routes_keys = jax.random.split(jax.random.fold_in(key_list[2], 1), TOKENS // TOK_DEV)
    routes_turns = jax.random.permutation(jax.random.fold_in(key_list[2], 3), TOKENS // TOK_DEV)
    routes = jax.vmap(lambda own, number: assign_block(jax.random.fold_in(key_list[2], 2), own, number, TOK_DEV, EXPERTS, TOP, CAP, 2))(routes_keys, routes_turns).reshape((TOKENS, TOP))
    cotangent = gaussian(key_list[3], (TOKENS, D), 1.0, 6.0, ((0, 512),))
    old_home = jax.random.permutation(key_list[4], EXPERTS).astype(jnp.int32)
    swap_flags = plant((jax.random.randint(key_list[5], (PAIRS,), 0, 2) < 1).astype(jnp.int32), jax.random.fold_in(key_list[5], 1), 0, 1)
    weights = gaussian(key_list[6], (EXPERTS, 3, FF, D), FF ** -0.5, 0.3125, ((0, 64), (2, 8)))
    first_moment = gaussian(key_list[7], (EXPERTS, 3, FF, D), 3.0, 18.0, ((0, 64), (2, 8)), jnp.float32)
    second_moment = jnp.clip(jnp.exp(math.log(1000.0) - 6.9077553 * jax.random.uniform(key_list[8], (EXPERTS, 3, FF, D), jnp.float32) ** level_of(key_list[8], (EXPERTS, 3, FF, D), ((0, 64), (2, 8)), -0.2, 0.2)), 1.0, 1000.0)
    return {"tokens": tokens, "gates": gates, "routes": routes, "cotangent": cotangent, "old_home": old_home, "swap_flags": swap_flags, "weights": weights, "first_moment": first_moment, "second_moment": second_moment}


BETA_ONE = 0.9
BETA_TWO = 0.95
LEARN_RATE = 0.001
EPSILON = 1e-08
STEP_COUNT = 20.0

def reference(tokens, gates, routes, cotangent, old_home, swap_flags, weights, first_moment, second_moment):
    slot_numbers = jnp.arange(EXPERTS, dtype=jnp.int32)
    partner = (slot_numbers + PAIRS) % EXPERTS
    flag_rows = jnp.concatenate([swap_flags, swap_flags])
    source = jnp.where(flag_rows == 1, partner, slot_numbers)
    new_home = old_home[source]
    slot_of = jnp.zeros((EXPERTS,), jnp.int32).at[new_home].set(slot_numbers)
    blocks = TOKENS // TOK_DEV
    flat = routes.reshape(blocks, TOK_DEV * TOP)
    indicator_matrix = (flat[:, :, None] == slot_numbers[None, None, :]).astype(jnp.int32)
    before = jnp.cumsum(indicator_matrix, axis=1) - indicator_matrix
    rank = lax.optimization_barrier(jnp.sum(before * indicator_matrix, axis=2)).reshape(TOKENS, TOP)
    target = slot_of[routes]
    block_id = jnp.arange(TOKENS, dtype=jnp.int32) // TOK_DEV
    row_pos = (block_id % N_TP * N_EP + block_id // N_TP)[:, None] * CAP + rank
    token_id = jnp.broadcast_to(jnp.arange(TOKENS, dtype=jnp.int32)[:, None], (TOKENS, TOP))
    rows = N_TP * N_EP * CAP

    def one_slot(carry, slot):
        out_sum, grad_sum = carry
        place = jnp.where(target == slot, row_pos, rows).reshape(-1)
        token_index = jnp.zeros((rows,), jnp.int32).at[place].set(token_id.reshape(-1), mode='drop')
        valid = jnp.zeros((rows,), jnp.float32).at[place].set(1.0, mode='drop')
        gate_row = jnp.zeros((rows,), jnp.float32).at[place].set(gates.reshape(-1), mode='drop')
        live = valid[:, None] > 0
        x_rows = jnp.where(live, tokens[token_index], jnp.zeros((), jnp.bfloat16))
        upstream_rows = (gate_row[:, None] * cotangent[token_index].astype(jnp.float32)).astype(jnp.bfloat16)
        anchor = source[slot]
        expert_w = lax.dynamic_index_in_dim(weights, anchor, 0, keepdims=False)
        inner = expert_w[:2].reshape(2 * FF, D)
        projected = jnp.dot(x_rows, inner.T, preferred_element_type=jnp.float32)
        gate_pre = projected[:, :FF]
        up_pre = projected[:, FF:]
        sigmoid_gate = jax.nn.sigmoid(gate_pre)
        hidden = (gate_pre * sigmoid_gate * up_pre).astype(jnp.bfloat16)
        expert_out = jnp.dot(hidden, expert_w[2], preferred_element_type=jnp.float32).astype(jnp.bfloat16)
        hidden_grad = jnp.dot(upstream_rows, expert_w[2].T, preferred_element_type=jnp.float32)
        gate_grad = hidden_grad * up_pre * sigmoid_gate * (1.0 + gate_pre * (1.0 - sigmoid_gate))
        up_grad = hidden_grad * gate_pre * sigmoid_gate
        projected_grad = jnp.concatenate([gate_grad, up_grad], axis=1).astype(jnp.bfloat16)
        row_grad = jnp.dot(projected_grad, inner, preferred_element_type=jnp.float32).astype(jnp.bfloat16)
        out_sum = out_sum.at[token_index].add(gate_row[:, None] * expert_out.astype(jnp.float32))
        grad_sum = grad_sum.at[token_index].add(valid[:, None] * row_grad.astype(jnp.float32))
        x_three = x_rows.astype(jnp.float32).reshape(N_TP, -1, D)
        up_projection_cube = upstream_rows.astype(jnp.float32).reshape(N_TP, -1, D)
        pg_three = projected_grad.astype(jnp.float32).reshape(N_TP, -1, 2 * FF)
        hidden_cube = hidden.astype(jnp.float32).reshape(N_TP, -1, FF)
        grad_inner = jnp.einsum('trg,trd->tgd', pg_three, x_three, precision=lax.Precision.HIGHEST)
        down_projection_gradient = jnp.einsum('ksa,kso->kao', hidden_cube, up_projection_cube, precision=lax.Precision.HIGHEST)
        partial_grad = jnp.concatenate([grad_inner.reshape(N_TP, 2, FF, D), down_projection_gradient[:, None]], axis=1)
        partial_grad = partial_grad.astype(jnp.bfloat16).astype(jnp.float32)
        gradient = lax.optimization_barrier(jnp.sum(partial_grad, axis=0))
        moment_one = lax.dynamic_index_in_dim(first_moment, anchor, 0, keepdims=False)
        moment_two = lax.dynamic_index_in_dim(second_moment, anchor, 0, keepdims=False)
        first_new = BETA_ONE * moment_one + (1.0 - BETA_ONE) * gradient
        second_new = BETA_TWO * moment_two + (1.0 - BETA_TWO) * gradient * gradient
        adam_step = LEARN_RATE * (first_new / (1.0 - BETA_ONE ** STEP_COUNT)) / (jnp.sqrt(second_new / (1.0 - BETA_TWO ** STEP_COUNT)) + EPSILON)
        weight_new = (expert_w.astype(jnp.float32) - adam_step).astype(jnp.bfloat16)
        return ((out_sum, grad_sum), (weight_new, first_new, second_new))
    start_carry = (jnp.zeros((TOKENS, D), jnp.float32), jnp.zeros((TOKENS, D), jnp.float32))
    (out_sum, grad_sum), (new_weights, new_first, new_second) = lax.scan(one_slot, start_carry, slot_numbers)
    return (out_sum.astype(jnp.bfloat16), grad_sum.astype(jnp.bfloat16), new_weights, new_first, new_second)
```

```python
import jax
import jax.numpy as jnp
from jax import lax
from jax.experimental import pallas as pl
from jax.experimental.pallas import tpu as pltpu
from jax.sharding import PartitionSpec as P

BETA_ONE = 0.9
BETA_TWO = 0.95
LEARN_RATE = 0.001
EPSILON = 1e-08
STEP_COUNT = 20.0

VMEM_LIMIT = 40 * 1024 * 1024


def partner(array, axis, apart):
    return lax.ppermute(array, axis, [(i, i ^ 1 << apart) for i in range(lax.axis_size(axis))])


def dot_first(a, b):
    return lax.dot_general(a, b, (((0,), (0,)), ((), ())), preferred_element_type=jnp.float32)


def dispatch_kernel(routes_ref, gates_ref, home_ref, tokens_ref, cotangent_ref,
                    send_x_ref, send_g_ref, place_ref, weigh_ref):
    tok_rows, top_count = routes_ref.shape
    slot_count = home_ref.shape[1]
    buffer_rows = send_x_ref.shape[0]
    capacity = buffer_rows // slot_count
    home = home_ref[...]
    named = jnp.zeros((tok_rows, slot_count), jnp.float32)
    gate = jnp.zeros((tok_rows, slot_count), jnp.float32)
    for k in range(top_count):
        hit = routes_ref[:, k : k + 1] == home
        named = named + jnp.where(hit, 1.0, 0.0)
        gate = gate + jnp.where(hit, gates_ref[:, k : k + 1], 0.0)
    row = lax.broadcasted_iota(jnp.int32, (tok_rows, tok_rows), 0)
    col = lax.broadcasted_iota(jnp.int32, (tok_rows, tok_rows), 1)
    earlier = jnp.where(col < row, 1.0, 0.0).astype(jnp.bfloat16)
    rank = jnp.dot(earlier, named.astype(jnp.bfloat16), preferred_element_type=jnp.float32)
    rank = jnp.where(named > 0, rank, -1.0)
    slot = lax.broadcasted_iota(jnp.int32, (slot_count, buffer_rows), 0)
    place = lax.broadcasted_iota(jnp.int32, (slot_count, buffer_rows), 1)
    spread = jnp.where(place // capacity == slot, 1.0, 0.0).astype(jnp.bfloat16)

    def widen(values):
        return jnp.dot(values.astype(jnp.bfloat16), spread, preferred_element_type=jnp.float32)

    gate_high = gate.astype(jnp.bfloat16).astype(jnp.float32)
    gate_low = gate - gate_high
    place = lax.broadcasted_iota(jnp.int32, (tok_rows, buffer_rows), 1)
    hit = widen(rank) == (place % capacity).astype(jnp.float32)
    one = jnp.where(hit, 1.0, 0.0).astype(jnp.bfloat16)
    high = jnp.where(hit, widen(gate_high), 0.0).astype(jnp.bfloat16)
    low = jnp.where(hit, widen(gate_low), 0.0).astype(jnp.bfloat16)
    place_ref[...] = one
    weigh_ref[:, :buffer_rows] = high
    weigh_ref[:, buffer_rows:] = low
    send_x_ref[...] = dot_first(one, tokens_ref[...]).astype(jnp.bfloat16)
    cotangent = cotangent_ref[...]
    send_g_ref[...] = (dot_first(high, cotangent) + dot_first(low, cotangent)).astype(jnp.bfloat16)


def dispatch(routes, gates, home, tokens, cotangent):
    tok_rows, model_width = tokens.shape
    buffer_rows = tok_rows * routes.shape[1]
    return pl.pallas_call(
        dispatch_kernel,
        out_shape=(
            jax.ShapeDtypeStruct((buffer_rows, model_width), jnp.bfloat16),
            jax.ShapeDtypeStruct((buffer_rows, model_width), jnp.bfloat16),
            jax.ShapeDtypeStruct((tok_rows, buffer_rows), jnp.bfloat16),
            jax.ShapeDtypeStruct((tok_rows, 2 * buffer_rows), jnp.bfloat16),
        ),
        compiler_params=pltpu.CompilerParams(vmem_limit_bytes=VMEM_LIMIT),
    )(routes, gates, home, tokens, cotangent)


def expert_forward(x_rows, gathered):
    hidden_width = gathered.shape[1]
    model_width = gathered.shape[2]
    inner = gathered[:2].reshape(2 * hidden_width, model_width)
    projected = jnp.einsum("rd,gd->rg", x_rows, inner, preferred_element_type=jnp.float32)
    gate_pre = projected[:, :hidden_width]
    up_pre = projected[:, hidden_width:]
    sigmoid_gate = jax.nn.sigmoid(gate_pre)
    hidden = (gate_pre * sigmoid_gate * up_pre).astype(jnp.bfloat16)
    expert_out = jnp.dot(hidden, gathered[2], preferred_element_type=jnp.float32).astype(
        jnp.bfloat16
    )
    return (hidden, gate_pre, up_pre, sigmoid_gate, expert_out)


def expert_backward(upstream_rows, gathered, gate_pre, up_pre, sigmoid_gate):
    hidden_width = gathered.shape[1]
    model_width = gathered.shape[2]
    inner = gathered[:2].reshape(2 * hidden_width, model_width)
    hidden_grad = jnp.einsum(
        "rd,fd->rf", upstream_rows, gathered[2], preferred_element_type=jnp.float32
    )
    gate_grad = hidden_grad * up_pre * sigmoid_gate * (1.0 + gate_pre * (1.0 - sigmoid_gate))
    up_grad = hidden_grad * gate_pre * sigmoid_gate
    projected_grad = jnp.concatenate([gate_grad, up_grad], axis=1).astype(jnp.bfloat16)
    row_grad = jnp.dot(projected_grad, inner, preferred_element_type=jnp.float32).astype(
        jnp.bfloat16
    )
    return (projected_grad, row_grad)


def adam_update(weights, first_moment, second_moment, gradient):
    first_new = BETA_ONE * first_moment + (1.0 - BETA_ONE) * gradient
    second_new = BETA_TWO * second_moment + (1.0 - BETA_TWO) * gradient * gradient
    adam_step = (
        LEARN_RATE
        * (first_new / (1.0 - BETA_ONE**STEP_COUNT))
        / (jnp.sqrt(second_new / (1.0 - BETA_TWO**STEP_COUNT)) + EPSILON)
    )
    weight_new = (weights.astype(jnp.float32) - adam_step).astype(jnp.bfloat16)
    return (weight_new, first_new, second_new)


def shards(
    tokens, gates, routes, cotangent, old_home, swap_flags, weights, first_moment, second_moment
):
    slot_count = lax.axis_size("ep")
    top_bit = slot_count.bit_length() - 2
    own = lax.axis_index("ep")
    model_width = tokens.shape[1]
    flag_rows = jnp.concatenate([swap_flags, swap_flags])
    is_swapped = jnp.sum(jnp.where(jnp.arange(slot_count) == own, flag_rows, 0)) == 1

    def exchange(rows):
        rows = rows.reshape(slot_count, -1, model_width)
        rows = lax.all_to_all(rows, "ep", split_axis=0, concat_axis=0, tiled=True)
        return rows.reshape(-1, model_width)

    weights = jnp.where(is_swapped, partner(weights, "ep", top_bit), weights)
    gathered = lax.all_gather(weights[0], "tp", axis=1, tiled=True)
    new_home = jnp.where(flag_rows == 1, jnp.roll(old_home, -(slot_count // 2)), old_home)
    send_x, send_g, place, weigh = dispatch(
        routes, gates, new_home.reshape(1, -1), tokens, cotangent
    )
    x_rows = exchange(send_x)
    upstream_rows = exchange(send_g)
    hidden, gate_pre, up_pre, sigmoid_gate, expert_out = expert_forward(x_rows, gathered)
    back_out = exchange(expert_out)
    projected_grad, row_grad = expert_backward(
        upstream_rows, gathered, gate_pre, up_pre, sigmoid_gate
    )
    back_grad = exchange(row_grad)

    hidden_width = hidden.shape[1]
    down_terms = dot_first(hidden, upstream_rows).astype(jnp.bfloat16)[None]
    inner_terms = dot_first(projected_grad, x_rows).astype(jnp.bfloat16)
    inner_terms = inner_terms.reshape(2, hidden_width, model_width)
    down_sum = lax.psum_scatter(down_terms, "tp", scatter_dimension=1, tiled=True)
    inner_sum = lax.psum_scatter(inner_terms, "tp", scatter_dimension=1, tiled=True)
    gradient = jnp.concatenate([inner_sum, down_sum], axis=0)[None]

    other_first = partner(first_moment.astype(jnp.bfloat16), "ep", top_bit)
    other_second = partner(second_moment.astype(jnp.bfloat16), "ep", top_bit)
    first_moment = jnp.where(is_swapped, other_first.astype(jnp.float32), first_moment)
    second_moment = jnp.where(is_swapped, other_second.astype(jnp.float32), second_moment)
    gradient = gradient.astype(jnp.float32)
    new_weights, new_first, new_second = adam_update(weights, first_moment, second_moment, gradient)

    buffer_rows = place.shape[1]
    layer_output_rows = (
        jnp.dot(weigh[:, :buffer_rows], back_out, preferred_element_type=jnp.float32)
        + jnp.dot(weigh[:, buffer_rows:], back_out, preferred_element_type=jnp.float32)
    ).astype(jnp.bfloat16)
    token_gradient_rows = jnp.dot(place, back_grad, preferred_element_type=jnp.float32).astype(
        jnp.bfloat16
    )
    return (layer_output_rows, token_gradient_rows, new_weights, new_first, new_second)


def solution(mesh):
    in_specs = (
        P(("ep", "tp"), None),
        P(("ep", "tp"), None),
        P(("ep", "tp"), None),
        P(("ep", "tp"), None),
        P(),
        P(),
        P("ep", None, "tp", None),
        P("ep", None, "tp", None),
        P("ep", None, "tp", None),
    )
    out_specs = (
        P(("ep", "tp"), None),
        P(("ep", "tp"), None),
        P("ep", None, "tp", None),
        P("ep", None, "tp", None),
        P("ep", None, "tp", None),
    )
    return jax.shard_map(shards, mesh=mesh, in_specs=in_specs, out_specs=out_specs, check_vma=False)
```

```python
import jax
import jax.numpy as jnp
from jax import lax
from jax.experimental import pallas as pl
from jax.experimental.pallas import tpu as pltpu
from jax.sharding import PartitionSpec as P

BETA_ONE = 0.9
BETA_TWO = 0.95
LEARN_RATE = 0.001
EPSILON = 1e-08
STEP_COUNT = 20.0

X_SIZE = 4
VMEM_LIMIT = 60 * 1024 * 1024
PARAMS = pltpu.CompilerParams(vmem_limit_bytes=VMEM_LIMIT)


def partner(array, apart):
    return lax.ppermute(array, "ep", [(i, i ^ apart) for i in range(lax.axis_size("ep"))])


def dot(a, b):
    return jnp.dot(a, b, preferred_element_type=jnp.float32)


def dot_last(a, b):
    return lax.dot_general(a, b, (((1,), (1,)), ((), ())), preferred_element_type=jnp.float32)


def dot_first(a, b):
    return lax.dot_general(a, b, (((0,), (0,)), ((), ())), preferred_element_type=jnp.float32)


def iota(shape, axis):
    return lax.broadcasted_iota(jnp.int32, shape, axis)


def route_kernel(pack_ref, home_ref, flags_ref, tokens_ref, cotangent_ref, send_ref, mats_ref):
    top_count = pack_ref.shape[0] // 2
    tok_rows = pack_ref.shape[1]
    slot_count = home_ref.shape[1]
    pairs = slot_count // 2
    half = slot_count // 2
    rows = send_ref.shape[0]
    capacity = rows // half // 2
    z_half = lax.axis_index("ep") // X_SIZE % 2
    place = iota((half, 1), 0)
    slot = (place // X_SIZE * 2 + z_half) * X_SIZE + place % X_SIZE
    flag = jnp.sum(
        jnp.where(iota((half, pairs), 1) == slot % pairs, flags_ref[...].astype(jnp.float32), 0.0),
        axis=1,
        keepdims=True,
    )
    source = jnp.where(flag > 0, (slot + pairs) % slot_count, slot)
    expert = jnp.sum(
        jnp.where(iota((half, slot_count), 1) == source, home_ref[...].astype(jnp.float32), 0.0),
        axis=1,
        keepdims=True,
    )
    named = jnp.zeros((half, tok_rows), jnp.float32)
    gate = jnp.zeros((half, tok_rows), jnp.float32)
    for k in range(top_count):
        hit = pack_ref[k : k + 1, :] == expert
        named = named + jnp.where(hit, 1.0, 0.0)
        gate = gate + jnp.where(hit, pack_ref[top_count + k : top_count + k + 1, :], 0.0)
    earlier = iota((tok_rows, tok_rows), 0) < iota((tok_rows, tok_rows), 1)
    earlier = jnp.where(earlier, 1.0, 0.0).astype(jnp.bfloat16)
    rank = jnp.where(named > 0, dot(named.astype(jnp.bfloat16), earlier), -1.0)
    spread = iota((rows, half), 0) // (2 * capacity) == iota((rows, half), 1)
    spread = jnp.where(spread, 1.0, 0.0).astype(jnp.bfloat16)
    gate_high = gate.astype(jnp.bfloat16)
    gate_low = (gate - gate_high.astype(jnp.float32)).astype(jnp.bfloat16)
    row = iota((rows, 1), 0)
    hit = dot(spread, rank.astype(jnp.bfloat16)) == (row % capacity).astype(jnp.float32)
    first = row // capacity % 2 == 0
    high = dot(spread, gate_high)
    low = dot(spread, gate_low)

    def pick(values, kind):
        return jnp.where(hit & kind, values, 0.0).astype(jnp.bfloat16)

    second = jnp.logical_not(first)
    mats_ref[0] = pick(high, first)
    mats_ref[1] = pick(low, first)
    mats_ref[2] = pick(1.0, second)
    cotangent = cotangent_ref[...]
    send_ref[...] = (
        dot(pick(1.0, first), tokens_ref[...])
        + dot(pick(high, second), cotangent)
        + dot(pick(low, second), cotangent)
    ).astype(jnp.bfloat16)


def route(pack, home, flags, tokens, cotangent):
    tok_rows, model_width = tokens.shape
    rows = tok_rows * (pack.shape[0] // 2)
    return pl.pallas_call(
        route_kernel,
        out_shape=(
            jax.ShapeDtypeStruct((rows, model_width), jnp.bfloat16),
            jax.ShapeDtypeStruct((3, rows, tok_rows), jnp.bfloat16),
        ),
        compiler_params=PARAMS,
        name="route",
    )(pack, home, flags, tokens, cotangent)


def expert_kernel(arrived_ref, weights_ref, back_ref, act_ref):
    sources, double, width = arrived_ref.shape
    capacity = double // 2
    hidden_width = weights_ref.shape[1]
    x_rows = arrived_ref[:, :capacity, :].reshape(sources * capacity, width)
    upstream = arrived_ref[:, capacity:, :].reshape(sources * capacity, width)
    w_gate, w_up, w_down = weights_ref[0], weights_ref[1], weights_ref[2]
    gate_pre = dot_last(x_rows, w_gate)
    up_pre = dot_last(x_rows, w_up)
    sigmoid = jax.nn.sigmoid(gate_pre)
    hidden = (gate_pre * sigmoid * up_pre).astype(jnp.bfloat16)
    out = dot(hidden, w_down).astype(jnp.bfloat16)
    back_ref[:, :capacity, :] = out.reshape(sources, capacity, width)
    hidden_grad = dot_last(upstream, w_down)
    gate_grad = hidden_grad * up_pre * sigmoid * (1.0 + gate_pre * (1.0 - sigmoid))
    gate_grad = gate_grad.astype(jnp.bfloat16)
    up_grad = (hidden_grad * gate_pre * sigmoid).astype(jnp.bfloat16)
    row_grad = (dot(gate_grad, w_gate) + dot(up_grad, w_up)).astype(jnp.bfloat16)
    back_ref[:, capacity:, :] = row_grad.reshape(sources, capacity, width)
    act_ref[:, :hidden_width] = gate_grad
    act_ref[:, hidden_width : 2 * hidden_width] = up_grad
    act_ref[:, 2 * hidden_width :] = hidden


def expert(arrived, weights, steps):
    sources, double, width = arrived.shape
    hidden_width = weights.shape[1]
    block = sources // steps
    rows = block * double // 2
    return pl.pallas_call(
        expert_kernel,
        grid=(steps,),
        in_specs=[
            pl.BlockSpec((block, double, width), lambda i: (i, 0, 0)),
            pl.BlockSpec((3, hidden_width, width), lambda i: (0, 0, 0)),
        ],
        out_specs=(
            pl.BlockSpec((block, double, width), lambda i: (i, 0, 0)),
            pl.BlockSpec((rows, 3 * hidden_width), lambda i: (i, 0)),
        ),
        out_shape=(
            jax.ShapeDtypeStruct(arrived.shape, jnp.bfloat16),
            jax.ShapeDtypeStruct((rows * steps, 3 * hidden_width), jnp.bfloat16),
        ),
        compiler_params=PARAMS,
        name="expert",
    )(arrived, weights)


def terms_kernel(one_ref, one_act_ref, two_ref, two_act_ref, terms_ref):
    sources, double, width = one_ref.shape
    capacity = double // 2
    inner = terms_ref.shape[0] // 3 * 2

    def kind(ref, low):
        return ref[:, low : low + capacity, :].reshape(sources * capacity, width)

    terms_ref[:inner] = (
        dot_first(one_act_ref[:, :inner], kind(one_ref, 0))
        + dot_first(two_act_ref[:, :inner], kind(two_ref, 0))
    ).astype(jnp.bfloat16)
    terms_ref[inner:] = (
        dot_first(one_act_ref[:, inner:], kind(one_ref, capacity))
        + dot_first(two_act_ref[:, inner:], kind(two_ref, capacity))
    ).astype(jnp.bfloat16)


def gradient_terms(one, one_act, two, two_act):
    return pl.pallas_call(
        terms_kernel,
        out_shape=jax.ShapeDtypeStruct((one_act.shape[1], one.shape[2]), jnp.bfloat16),
        compiler_params=PARAMS,
        name="terms",
    )(one, one_act, two, two_act)


def share_kernel(back_ref, mats_ref, share_ref):
    back = back_ref[...]
    tok_rows = mats_ref.shape[2]
    out = dot_first(mats_ref[0], back) + dot_first(mats_ref[1], back)
    share_ref[:tok_rows] = out.astype(jnp.bfloat16)
    share_ref[tok_rows:] = dot_first(mats_ref[2], back).astype(jnp.bfloat16)


def share(back, mats):
    return pl.pallas_call(
        share_kernel,
        out_shape=jax.ShapeDtypeStruct((2 * mats.shape[2], back.shape[1]), jnp.bfloat16),
        compiler_params=PARAMS,
        name="share",
    )(back, mats)


def combine_kernel(back_ref, mats_ref, share_ref, out_ref, grad_ref):
    back = back_ref[...]
    tok_rows = mats_ref.shape[2]
    out = dot_first(mats_ref[0], back) + dot_first(mats_ref[1], back)
    out_ref[...] = (out + share_ref[:tok_rows].astype(jnp.float32)).astype(jnp.bfloat16)
    grad = dot_first(mats_ref[2], back)
    grad_ref[...] = (grad + share_ref[tok_rows:].astype(jnp.float32)).astype(jnp.bfloat16)


def combine(back, mats, other_share):
    shape = jax.ShapeDtypeStruct((mats.shape[2], back.shape[1]), jnp.bfloat16)
    return pl.pallas_call(
        combine_kernel,
        out_shape=(shape, shape),
        compiler_params=PARAMS,
        name="combine",
    )(back, mats, other_share)


def adam_update(weights, first_moment, second_moment, gradient):
    first_new = BETA_ONE * first_moment + (1.0 - BETA_ONE) * gradient
    second_new = BETA_TWO * second_moment + (1.0 - BETA_TWO) * gradient * gradient
    adam_step = (
        LEARN_RATE
        * (first_new / (1.0 - BETA_ONE**STEP_COUNT))
        / (jnp.sqrt(second_new / (1.0 - BETA_TWO**STEP_COUNT)) + EPSILON)
    )
    weight_new = (weights.astype(jnp.float32) - adam_step).astype(jnp.bfloat16)
    return (weight_new, first_new, second_new)


def shards(
    tokens, gates, routes, cotangent, old_home, swap_flags, weights, first_moment, second_moment
):
    slot_count = lax.axis_size("ep")
    half = slot_count // 2
    own = lax.axis_index("ep")
    model_width = tokens.shape[1]
    hidden_width = weights.shape[2] * lax.axis_size("tp")
    is_swapped = jnp.sum(jnp.where(jnp.arange(half) == own % half, swap_flags, 0)) == 1
    groups = [
        [i for i in range(slot_count) if i // X_SIZE % 2 == z_half] for z_half in range(2)
    ]

    def exchange(rows):
        rows = rows.reshape(half, -1, model_width)
        return lax.all_to_all(
            rows, "ep", split_axis=0, concat_axis=0, tiled=True, axis_index_groups=groups
        )

    home = old_home.reshape(1, -1)
    flags = swap_flags.reshape(1, -1)
    pack = jnp.concatenate([routes.T.astype(jnp.float32), gates.T], axis=0)
    own_send, own_mats = route(pack, home, flags, tokens, cotangent)
    own_arrived = exchange(own_send)
    both = jnp.concatenate([tokens, cotangent], axis=0)
    pack, both, _ = lax.optimization_barrier((pack, both, own_send))
    other_pack, both = partner(pack, X_SIZE), partner(both, X_SIZE)
    tok_rows = tokens.shape[0]
    other_send, other_mats = route(other_pack, home, flags, both[:tok_rows], both[tok_rows:])
    first_sent, second_sent = first_moment.astype(jnp.bfloat16), second_moment.astype(jnp.bfloat16)
    other_send, own_arrived, first_sent = lax.optimization_barrier(
        (other_send, own_arrived, first_sent)
    )
    other_first = partner(first_sent, half)
    other_arrived = exchange(other_send)

    weights = jnp.where(is_swapped, partner(weights, half), weights)
    gathered = lax.all_gather(weights[0], "tp", axis=1, tiled=True)
    own_back, own_act = expert(own_arrived, gathered, 2)
    other_arrived, own_back, own_act, other_first, second_sent = lax.optimization_barrier(
        (other_arrived, own_back, own_act, other_first, second_sent)
    )
    other_second = partner(second_sent, half)
    other_back, other_act = expert(other_arrived, gathered, 2)
    other_returned = exchange(other_back)
    own_back, other_returned, other_second = lax.optimization_barrier(
        (own_back, other_returned, other_second)
    )
    own_returned = exchange(own_back).reshape(-1, model_width)
    other_returned = other_returned.reshape(-1, model_width)

    terms = gradient_terms(own_arrived, own_act, other_arrived, other_act)
    terms = terms.reshape(3, hidden_width, model_width)
    gradient = lax.psum_scatter(terms, "tp", scatter_dimension=1, tiled=True)
    gradient = gradient[None].astype(jnp.float32)
    first_moment = jnp.where(is_swapped, other_first.astype(jnp.float32), first_moment)
    second_moment = jnp.where(is_swapped, other_second.astype(jnp.float32), second_moment)
    new_weights, new_first, new_second = adam_update(weights, first_moment, second_moment, gradient)

    other_share = partner(share(other_returned, other_mats), X_SIZE)
    layer_output_rows, token_gradient_rows = combine(own_returned, own_mats, other_share)
    return (layer_output_rows, token_gradient_rows, new_weights, new_first, new_second)


def solution(mesh):
    in_specs = (
        P(("ep", "tp"), None),
        P(("ep", "tp"), None),
        P(("ep", "tp"), None),
        P(("ep", "tp"), None),
        P(),
        P(),
        P("ep", None, "tp", None),
        P("ep", None, "tp", None),
        P("ep", None, "tp", None),
    )
    out_specs = (
        P(("ep", "tp"), None),
        P(("ep", "tp"), None),
        P("ep", None, "tp", None),
        P("ep", None, "tp", None),
        P("ep", None, "tp", None),
    )
    return jax.shard_map(shards, mesh=mesh, in_specs=in_specs, out_specs=out_specs, check_vma=False)
```

```python
import jax
import jax.numpy as jnp
from jax import lax
from jax.experimental import pallas as pl
from jax.experimental.pallas import tpu as pltpu
from jax.sharding import PartitionSpec as P

BETA_ONE = 0.9
BETA_TWO = 0.95
LEARN_RATE = 0.001
EPSILON = 1e-08
STEP_COUNT = 20.0

X_SIZE = 4
VMEM_LIMIT = 60 * 1024 * 1024
COST = {"route_own": 30, "route_other": 30, "expert_own": 100, "expert_other": 10, "terms": 30, "share": 10, "combine": 10}
PARAMS = pltpu.CompilerParams(vmem_limit_bytes=VMEM_LIMIT)


def cost(name):
    return pl.CostEstimate(flops=COST[name] * 10**9, bytes_accessed=0, transcendentals=0)


def partner(array, apart):
    return lax.ppermute(array, "ep", [(i, i ^ apart) for i in range(lax.axis_size("ep"))])


def dot(a, b):
    return jnp.dot(a, b, preferred_element_type=jnp.float32)


def dot_last(a, b):
    return lax.dot_general(a, b, (((1,), (1,)), ((), ())), preferred_element_type=jnp.float32)


def dot_first(a, b):
    return lax.dot_general(a, b, (((0,), (0,)), ((), ())), preferred_element_type=jnp.float32)


def iota(shape, axis):
    return lax.broadcasted_iota(jnp.int32, shape, axis)


def route_kernel(pack_ref, home_ref, flags_ref, tokens_ref, cotangent_ref, send_ref, mats_ref):
    top_count = pack_ref.shape[0] // 2
    tok_rows = pack_ref.shape[1]
    slot_count = home_ref.shape[1]
    pairs = slot_count // 2
    half = slot_count // 2
    rows = send_ref.shape[0]
    capacity = rows // half // 2
    z_half = lax.axis_index("ep") // X_SIZE % 2
    place = iota((half, 1), 0)
    slot = (place // X_SIZE * 2 + z_half) * X_SIZE + place % X_SIZE
    flag = jnp.sum(
        jnp.where(iota((half, pairs), 1) == slot % pairs, flags_ref[...].astype(jnp.float32), 0.0),
        axis=1,
        keepdims=True,
    )
    source = jnp.where(flag > 0, (slot + pairs) % slot_count, slot)
    expert = jnp.sum(
        jnp.where(iota((half, slot_count), 1) == source, home_ref[...].astype(jnp.float32), 0.0),
        axis=1,
        keepdims=True,
    )
    named = jnp.zeros((half, tok_rows), jnp.float32)
    gate = jnp.zeros((half, tok_rows), jnp.float32)
    for k in range(top_count):
        hit = pack_ref[k : k + 1, :] == expert
        named = named + jnp.where(hit, 1.0, 0.0)
        gate = gate + jnp.where(hit, pack_ref[top_count + k : top_count + k + 1, :], 0.0)
    earlier = iota((tok_rows, tok_rows), 0) < iota((tok_rows, tok_rows), 1)
    earlier = jnp.where(earlier, 1.0, 0.0).astype(jnp.bfloat16)
    rank = jnp.where(named > 0, dot(named.astype(jnp.bfloat16), earlier), -1.0)
    spread = iota((rows, half), 0) // (2 * capacity) == iota((rows, half), 1)
    spread = jnp.where(spread, 1.0, 0.0).astype(jnp.bfloat16)
    gate_high = gate.astype(jnp.bfloat16)
    gate_low = (gate - gate_high.astype(jnp.float32)).astype(jnp.bfloat16)
    row = iota((rows, 1), 0)
    hit = dot(spread, rank.astype(jnp.bfloat16)) == (row % capacity).astype(jnp.float32)
    first = row // capacity % 2 == 0
    high = dot(spread, gate_high)
    low = dot(spread, gate_low)

    def pick(values, kind):
        return jnp.where(hit & kind, values, 0.0).astype(jnp.bfloat16)

    second = jnp.logical_not(first)
    mats_ref[0] = pick(high, first)
    mats_ref[1] = pick(low, first)
    mats_ref[2] = pick(1.0, second)
    cotangent = cotangent_ref[...]
    send_ref[...] = (
        dot(pick(1.0, first), tokens_ref[...])
        + dot(pick(high, second), cotangent)
        + dot(pick(low, second), cotangent)
    ).astype(jnp.bfloat16)


def route(pack, home, flags, tokens, cotangent, name):
    tok_rows, model_width = tokens.shape
    rows = tok_rows * (pack.shape[0] // 2)
    return pl.pallas_call(
        route_kernel,
        out_shape=(
            jax.ShapeDtypeStruct((rows, model_width), jnp.bfloat16),
            jax.ShapeDtypeStruct((3, rows, tok_rows), jnp.bfloat16),
        ),
        compiler_params=PARAMS,
        cost_estimate=cost(name),
        name=name,
    )(pack, home, flags, tokens, cotangent)


def expert_kernel(arrived_ref, weights_ref, back_ref, act_ref):
    sources, double, width = arrived_ref.shape
    capacity = double // 2
    hidden_width = weights_ref.shape[1]
    x_rows = arrived_ref[:, :capacity, :].reshape(sources * capacity, width)
    upstream = arrived_ref[:, capacity:, :].reshape(sources * capacity, width)
    w_gate, w_up, w_down = weights_ref[0], weights_ref[1], weights_ref[2]
    gate_pre = dot_last(x_rows, w_gate)
    up_pre = dot_last(x_rows, w_up)
    sigmoid = jax.nn.sigmoid(gate_pre)
    hidden = (gate_pre * sigmoid * up_pre).astype(jnp.bfloat16)
    out = dot(hidden, w_down).astype(jnp.bfloat16)
    back_ref[:, :capacity, :] = out.reshape(sources, capacity, width)
    hidden_grad = dot_last(upstream, w_down)
    gate_grad = hidden_grad * up_pre * sigmoid * (1.0 + gate_pre * (1.0 - sigmoid))
    gate_grad = gate_grad.astype(jnp.bfloat16)
    up_grad = (hidden_grad * gate_pre * sigmoid).astype(jnp.bfloat16)
    row_grad = (dot(gate_grad, w_gate) + dot(up_grad, w_up)).astype(jnp.bfloat16)
    back_ref[:, capacity:, :] = row_grad.reshape(sources, capacity, width)
    act_ref[:, :hidden_width] = gate_grad
    act_ref[:, hidden_width : 2 * hidden_width] = up_grad
    act_ref[:, 2 * hidden_width :] = hidden


def expert(arrived, weights, steps, name):
    sources, double, width = arrived.shape
    hidden_width = weights.shape[1]
    block = sources // steps
    rows = block * double // 2
    return pl.pallas_call(
        expert_kernel,
        grid=(steps,),
        in_specs=[
            pl.BlockSpec((block, double, width), lambda i: (i, 0, 0)),
            pl.BlockSpec((3, hidden_width, width), lambda i: (0, 0, 0)),
        ],
        out_specs=(
            pl.BlockSpec((block, double, width), lambda i: (i, 0, 0)),
            pl.BlockSpec((rows, 3 * hidden_width), lambda i: (i, 0)),
        ),
        out_shape=(
            jax.ShapeDtypeStruct(arrived.shape, jnp.bfloat16),
            jax.ShapeDtypeStruct((rows * steps, 3 * hidden_width), jnp.bfloat16),
        ),
        compiler_params=PARAMS,
        cost_estimate=cost(name),
        name=name,
    )(arrived, weights)


def terms_kernel(one_ref, one_act_ref, two_ref, two_act_ref, terms_ref):
    sources, double, width = one_ref.shape
    capacity = double // 2
    inner = terms_ref.shape[0] // 3 * 2

    def kind(ref, low):
        return ref[:, low : low + capacity, :].reshape(sources * capacity, width)

    terms_ref[:inner] = (
        dot_first(one_act_ref[:, :inner], kind(one_ref, 0))
        + dot_first(two_act_ref[:, :inner], kind(two_ref, 0))
    ).astype(jnp.bfloat16)
    terms_ref[inner:] = (
        dot_first(one_act_ref[:, inner:], kind(one_ref, capacity))
        + dot_first(two_act_ref[:, inner:], kind(two_ref, capacity))
    ).astype(jnp.bfloat16)


def gradient_terms(one, one_act, two, two_act):
    return pl.pallas_call(
        terms_kernel,
        out_shape=jax.ShapeDtypeStruct((one_act.shape[1], one.shape[2]), jnp.bfloat16),
        compiler_params=PARAMS,
        cost_estimate=cost("terms"),
        name="terms",
    )(one, one_act, two, two_act)


def share_kernel(back_ref, mats_ref, share_ref):
    back = back_ref[...]
    tok_rows = mats_ref.shape[2]
    out = dot_first(mats_ref[0], back) + dot_first(mats_ref[1], back)
    share_ref[:tok_rows] = out.astype(jnp.bfloat16)
    share_ref[tok_rows:] = dot_first(mats_ref[2], back).astype(jnp.bfloat16)


def share(back, mats):
    return pl.pallas_call(
        share_kernel,
        out_shape=jax.ShapeDtypeStruct((2 * mats.shape[2], back.shape[1]), jnp.bfloat16),
        compiler_params=PARAMS,
        cost_estimate=cost("share"),
        name="share",
    )(back, mats)


def combine_kernel(back_ref, mats_ref, share_ref, out_ref, grad_ref):
    back = back_ref[...]
    tok_rows = mats_ref.shape[2]
    out = dot_first(mats_ref[0], back) + dot_first(mats_ref[1], back)
    out_ref[...] = (out + share_ref[:tok_rows].astype(jnp.float32)).astype(jnp.bfloat16)
    grad = dot_first(mats_ref[2], back)
    grad_ref[...] = (grad + share_ref[tok_rows:].astype(jnp.float32)).astype(jnp.bfloat16)


def combine(back, mats, other_share):
    shape = jax.ShapeDtypeStruct((mats.shape[2], back.shape[1]), jnp.bfloat16)
    return pl.pallas_call(
        combine_kernel,
        out_shape=(shape, shape),
        compiler_params=PARAMS,
        cost_estimate=cost("combine"),
        name="combine",
    )(back, mats, other_share)


def adam_update(weights, first_moment, second_moment, gradient):
    first_new = BETA_ONE * first_moment + (1.0 - BETA_ONE) * gradient
    second_new = BETA_TWO * second_moment + (1.0 - BETA_TWO) * gradient * gradient
    adam_step = (
        LEARN_RATE
        * (first_new / (1.0 - BETA_ONE**STEP_COUNT))
        / (jnp.sqrt(second_new / (1.0 - BETA_TWO**STEP_COUNT)) + EPSILON)
    )
    weight_new = (weights.astype(jnp.float32) - adam_step).astype(jnp.bfloat16)
    return (weight_new, first_new, second_new)


def shards(
    tokens, gates, routes, cotangent, old_home, swap_flags, weights, first_moment, second_moment
):
    slot_count = lax.axis_size("ep")
    half = slot_count // 2
    own = lax.axis_index("ep")
    model_width = tokens.shape[1]
    hidden_width = weights.shape[2] * lax.axis_size("tp")
    is_swapped = jnp.sum(jnp.where(jnp.arange(half) == own % half, swap_flags, 0)) == 1
    groups = [
        [i for i in range(slot_count) if i // X_SIZE % 2 == z_half] for z_half in range(2)
    ]

    def exchange(rows):
        rows = rows.reshape(half, -1, model_width)
        return lax.all_to_all(
            rows, "ep", split_axis=0, concat_axis=0, tiled=True, axis_index_groups=groups
        )

    home = old_home.reshape(1, -1)
    flags = swap_flags.reshape(1, -1)
    pack = jnp.concatenate([routes.T.astype(jnp.float32), gates.T], axis=0)
    own_send, own_mats = route(pack, home, flags, tokens, cotangent, "route_own")
    own_arrived = exchange(own_send)
    weights = jnp.where(is_swapped, partner(weights, half), weights)
    gathered = lax.all_gather(weights[0], "tp", axis=1, tiled=True)
    both = jnp.concatenate([tokens, cotangent], axis=0)
    pack, both, _, _ = lax.optimization_barrier((pack, both, own_send, weights))
    other_pack, both = partner(pack, X_SIZE), partner(both, X_SIZE)
    tok_rows = tokens.shape[0]
    other_send, other_mats = route(other_pack, home, flags, both[:tok_rows], both[tok_rows:], "route_other")
    first_sent, second_sent = first_moment.astype(jnp.bfloat16), second_moment.astype(jnp.bfloat16)
    other_send, own_arrived, first_sent = lax.optimization_barrier(
        (other_send, own_arrived, first_sent)
    )
    other_first = partner(first_sent, half)
    other_arrived = exchange(other_send)

    own_arrived, other_first = lax.optimization_barrier((own_arrived, other_first))
    own_back, own_act = expert(own_arrived, gathered, 2, "expert_own")
    other_arrived, own_back, own_act, second_sent = lax.optimization_barrier(
        (other_arrived, own_back, own_act, second_sent)
    )
    other_second = partner(second_sent, half)
    other_back, other_act = expert(other_arrived, gathered, 2, "expert_other")
    other_returned = exchange(other_back)
    other_act, other_second = lax.optimization_barrier((other_act, other_second))
    own_back, other_returned = lax.optimization_barrier((own_back, other_returned))
    own_returned = exchange(own_back).reshape(-1, model_width)
    other_returned = other_returned.reshape(-1, model_width)

    terms = gradient_terms(own_arrived, own_act, other_arrived, other_act)
    terms = terms.reshape(3, hidden_width, model_width)
    gradient = lax.psum_scatter(terms, "tp", scatter_dimension=1, tiled=True)
    gradient = gradient[None].astype(jnp.float32)
    first_moment = jnp.where(is_swapped, other_first.astype(jnp.float32), first_moment)
    second_moment = jnp.where(is_swapped, other_second.astype(jnp.float32), second_moment)
    new_weights, new_first, new_second = adam_update(weights, first_moment, second_moment, gradient)

    other_share = partner(share(other_returned, other_mats), X_SIZE)
    layer_output_rows, token_gradient_rows = combine(own_returned, own_mats, other_share)
    return (layer_output_rows, token_gradient_rows, new_weights, new_first, new_second)


def solution(mesh):
    in_specs = (
        P(("ep", "tp"), None),
        P(("ep", "tp"), None),
        P(("ep", "tp"), None),
        P(("ep", "tp"), None),
        P(),
        P(),
        P("ep", None, "tp", None),
        P("ep", None, "tp", None),
        P("ep", None, "tp", None),
    )
    out_specs = (
        P(("ep", "tp"), None),
        P(("ep", "tp"), None),
        P("ep", None, "tp", None),
        P("ep", None, "tp", None),
        P("ep", None, "tp", None),
    )
    return jax.shard_map(shards, mesh=mesh, in_specs=in_specs, out_specs=out_specs, check_vma=False)
```

```python
import jax
import jax.numpy as jnp
from jax import lax
from jax.experimental import pallas as pl
from jax.experimental.pallas import tpu as pltpu
from jax.sharding import PartitionSpec as P

BETA_ONE = 0.9
BETA_TWO = 0.95
LEARN_RATE = 0.001
EPSILON = 1e-08
STEP_COUNT = 20.0

X_SIZE = 4
VMEM_LIMIT = 60 * 1024 * 1024
COST = {"route_own": 30, "route_other": 30, "expert_own": 27, "expert_other": 10, "terms": 30, "share": 40, "combine": 10, "assemble": 2, "pair": 2}
PARAMS = pltpu.CompilerParams(vmem_limit_bytes=VMEM_LIMIT)


def cost(name):
    return pl.CostEstimate(flops=COST[name] * 10**9, bytes_accessed=0, transcendentals=0)


def partner(array, apart):
    return lax.ppermute(array, "ep", [(i, i ^ apart) for i in range(lax.axis_size("ep"))])


def dot(a, b):
    return jnp.dot(a, b, preferred_element_type=jnp.float32)


def dot_last(a, b):
    return lax.dot_general(a, b, (((1,), (1,)), ((), ())), preferred_element_type=jnp.float32)


def dot_first(a, b):
    return lax.dot_general(a, b, (((0,), (0,)), ((), ())), preferred_element_type=jnp.float32)


def iota(shape, axis):
    return lax.broadcasted_iota(jnp.int32, shape, axis)


def route_kernel(routes_ref, gates_ref, home_ref, flags_ref, tokens_ref, cotangent_ref, send_ref, mats_ref):
    top_count, tok_rows = routes_ref.shape
    slot_count = home_ref.shape[1]
    pairs = slot_count // 2
    half, double, width = send_ref.shape
    capacity = double // 2
    rows = half * capacity
    z_half = lax.axis_index("ep") // X_SIZE % 2
    place = iota((half, 1), 0)
    slot = (place // X_SIZE * 2 + z_half) * X_SIZE + place % X_SIZE
    flag = jnp.sum(
        jnp.where(iota((half, pairs), 1) == slot % pairs, flags_ref[...].astype(jnp.float32), 0.0),
        axis=1,
        keepdims=True,
    )
    source = jnp.where(flag > 0, (slot + pairs) % slot_count, slot)
    expert = jnp.sum(
        jnp.where(iota((half, slot_count), 1) == source, home_ref[...].astype(jnp.float32), 0.0),
        axis=1,
        keepdims=True,
    )
    routes = routes_ref[...].astype(jnp.float32)
    named = jnp.zeros((half, tok_rows), jnp.float32)
    gate = jnp.zeros((half, tok_rows), jnp.float32)
    for k in range(top_count):
        hit = routes[k : k + 1, :] == expert
        named = named + jnp.where(hit, 1.0, 0.0)
        gate = gate + jnp.where(hit, gates_ref[k : k + 1, :], 0.0)
    earlier = iota((tok_rows, tok_rows), 0) < iota((tok_rows, tok_rows), 1)
    earlier = jnp.where(earlier, 1.0, 0.0).astype(jnp.bfloat16)
    rank = jnp.where(named > 0, dot(named.astype(jnp.bfloat16), earlier), -1.0)
    spread = iota((rows, half), 0) // capacity == iota((rows, half), 1)
    spread = jnp.where(spread, 1.0, 0.0).astype(jnp.bfloat16)
    gate_high = gate.astype(jnp.bfloat16)
    gate_low = (gate - gate_high.astype(jnp.float32)).astype(jnp.bfloat16)
    order = (iota((rows, 1), 0) % capacity).astype(jnp.float32)
    hit = dot(spread, rank.astype(jnp.bfloat16)) == order
    one = jnp.where(hit, 1.0, 0.0).astype(jnp.bfloat16)
    high = jnp.where(hit, dot(spread, gate_high), 0.0).astype(jnp.bfloat16)
    low = jnp.where(hit, dot(spread, gate_low), 0.0).astype(jnp.bfloat16)
    mats_ref[0] = high
    mats_ref[1] = low
    mats_ref[2] = one
    x_rows = dot(one, tokens_ref[...]).astype(jnp.bfloat16)
    send_ref[:, :capacity, :] = x_rows.reshape(half, capacity, width)
    cotangent = cotangent_ref[...]
    upstream = dot(
        jnp.concatenate([high, low], axis=1), jnp.concatenate([cotangent, cotangent], axis=0)
    ).astype(jnp.bfloat16)
    send_ref[:, capacity:, :] = upstream.reshape(half, capacity, width)


def route(routes, gates, home, flags, tokens, cotangent, name):
    top_count, tok_rows = routes.shape
    half = home.shape[1] // 2
    capacity = tok_rows * top_count // home.shape[1]
    return pl.pallas_call(
        route_kernel,
        out_shape=(
            jax.ShapeDtypeStruct((half, 2 * capacity, tokens.shape[1]), jnp.bfloat16),
            jax.ShapeDtypeStruct((3, half * capacity, tok_rows), jnp.bfloat16),
        ),
        compiler_params=PARAMS,
        cost_estimate=cost(name),
        name=name,
    )(routes, gates, home, flags, tokens, cotangent)


def expert_kernel(arrived_ref, weights_ref, back_ref, act_ref):
    sources, double, width = arrived_ref.shape
    capacity = double // 2
    hidden_width = weights_ref.shape[1]
    x_rows = arrived_ref[:, :capacity, :].reshape(sources * capacity, width)
    upstream = arrived_ref[:, capacity:, :].reshape(sources * capacity, width)
    inner = weights_ref[:2].reshape(2 * hidden_width, width)
    w_down = weights_ref[2]
    projected = dot_last(x_rows, inner)
    gate_pre = projected[:, :hidden_width]
    up_pre = projected[:, hidden_width:]
    sigmoid = jax.nn.sigmoid(gate_pre)
    hidden = (gate_pre * sigmoid * up_pre).astype(jnp.bfloat16)
    out = dot(hidden, w_down).astype(jnp.bfloat16)
    back_ref[:, :capacity, :] = out.reshape(sources, capacity, width)
    hidden_grad = dot_last(upstream, w_down)
    gate_grad = hidden_grad * up_pre * sigmoid * (1.0 + gate_pre * (1.0 - sigmoid))
    up_grad = hidden_grad * gate_pre * sigmoid
    act_ref[:, :hidden_width] = gate_grad.astype(jnp.bfloat16)
    act_ref[:, hidden_width : 2 * hidden_width] = up_grad.astype(jnp.bfloat16)
    act_ref[:, 2 * hidden_width :] = hidden
    row_grad = dot(act_ref[:, : 2 * hidden_width], inner).astype(jnp.bfloat16)
    back_ref[:, capacity:, :] = row_grad.reshape(sources, capacity, width)


def expert(arrived, weights, steps, name):
    sources, double, width = arrived.shape
    hidden_width = weights.shape[1]
    block = sources // steps
    rows = block * double // 2
    return pl.pallas_call(
        expert_kernel,
        grid=(steps,),
        in_specs=[
            pl.BlockSpec((block, double, width), lambda i: (i, 0, 0)),
            pl.BlockSpec((3, hidden_width, width), lambda i: (0, 0, 0)),
        ],
        out_specs=(
            pl.BlockSpec((block, double, width), lambda i: (i, 0, 0)),
            pl.BlockSpec((rows, 3 * hidden_width), lambda i: (i, 0)),
        ),
        out_shape=(
            jax.ShapeDtypeStruct(arrived.shape, jnp.bfloat16),
            jax.ShapeDtypeStruct((rows * steps, 3 * hidden_width), jnp.bfloat16),
        ),
        compiler_params=PARAMS,
        cost_estimate=cost(name),
        name=name,
    )(arrived, weights)


def terms_kernel(one_ref, one_act_ref, two_ref, two_act_ref, keep_ref, give_ref):
    sources, double, width = one_ref.shape
    capacity = double // 2
    matrices, half_width, _ = keep_ref.shape
    inner = (matrices - 1) * 2 * half_width

    def kind(ref, low):
        return ref[:, low : low + capacity, :].reshape(sources * capacity, width)

    def store(matrix, terms):
        keep_ref[matrix] = terms[:half_width]
        give_ref[matrix] = terms[half_width:]

    terms = (
        dot_first(one_act_ref[:, :inner], kind(one_ref, 0))
        + dot_first(two_act_ref[:, :inner], kind(two_ref, 0))
    ).astype(jnp.bfloat16)
    for matrix in range(matrices - 1):
        store(matrix, terms[matrix * 2 * half_width : (matrix + 1) * 2 * half_width])
    terms = (
        dot_first(one_act_ref[:, inner:], kind(one_ref, capacity))
        + dot_first(two_act_ref[:, inner:], kind(two_ref, capacity))
    ).astype(jnp.bfloat16)
    store(matrices - 1, terms)


def gradient_terms(one, one_act, two, two_act):
    shape = jax.ShapeDtypeStruct((3, one_act.shape[1] // 6, one.shape[2]), jnp.bfloat16)
    return pl.pallas_call(
        terms_kernel,
        out_shape=(shape, shape),
        compiler_params=PARAMS,
        cost_estimate=cost("terms"),
        name="terms",
    )(one, one_act, two, two_act)


def assemble_kernel(*refs):
    *shard_refs, other_ref, weights_ref = refs
    units = other_ref.shape[2]
    for place, ref in enumerate(shard_refs):
        weights_ref[:, place * units : (place + 1) * units, :] = ref[...]
    for dz in range(other_ref.shape[0]):
        place = len(shard_refs) + dz
        weights_ref[:, place * units : (place + 1) * units, :] = other_ref[dz]


def move_hidden(array, apart):
    return lax.ppermute(array, "tp", [(i, i ^ apart) for i in range(lax.axis_size("tp"))])


def gather_column(weights):
    return [weights] + [move_hidden(weights, 2 * dz) for dz in range(1, lax.axis_size("tp") // 2)]


def gather_hidden(shards):
    tp_count = lax.axis_size("tp")
    other = move_hidden(jnp.stack(shards), 1)
    matrices, units, width = shards[0].shape
    return pl.pallas_call(
        assemble_kernel,
        out_shape=jax.ShapeDtypeStruct((matrices, tp_count * units, width), jnp.bfloat16),
        compiler_params=PARAMS,
        cost_estimate=cost("assemble"),
        name="assemble",
    )(*shards, other)


def pair_kernel(keep_ref, given_ref, *sum_refs):
    units = sum_refs[0].shape[1]
    for dz, ref in enumerate(sum_refs):
        held = slice(dz * units, (dz + 1) * units)
        total = keep_ref[:, held, :].astype(jnp.float32) + given_ref[:, held, :].astype(jnp.float32)
        ref[...] = total.astype(jnp.bfloat16)


def core_sums(keep, give):
    given = move_hidden(give, 1)
    count = lax.axis_size("tp") // 2
    matrices, half_width, width = keep.shape
    shape = jax.ShapeDtypeStruct((matrices, half_width // count, width), jnp.bfloat16)
    return pl.pallas_call(
        pair_kernel,
        out_shape=[shape] * count,
        compiler_params=PARAMS,
        cost_estimate=cost("pair"),
        name="pair",
    )(keep, given)


def weighted_sums(back_ref, mats_ref):
    half, double, width = back_ref.shape
    capacity = double // 2
    out_rows = back_ref[:, :capacity, :].reshape(half * capacity, width)
    grad_rows = back_ref[:, capacity:, :].reshape(half * capacity, width)
    out = dot_first(mats_ref[0], out_rows) + dot_first(mats_ref[1], out_rows)
    return out, dot_first(mats_ref[2], grad_rows)


def share_kernel(back_ref, mats_ref, share_ref):
    tok_rows = mats_ref.shape[2]
    out, grad = weighted_sums(back_ref, mats_ref)
    share_ref[:tok_rows] = out.astype(jnp.bfloat16)
    share_ref[tok_rows:] = grad.astype(jnp.bfloat16)


def share(back, mats):
    return pl.pallas_call(
        share_kernel,
        out_shape=jax.ShapeDtypeStruct((2 * mats.shape[2], back.shape[2]), jnp.bfloat16),
        compiler_params=pltpu.CompilerParams(vmem_limit_bytes=24 * 1024 * 1024),
        cost_estimate=cost("share"),
        name="share",
    )(back, mats)


def combine_kernel(back_ref, mats_ref, share_ref, out_ref, grad_ref):
    tok_rows = mats_ref.shape[2]
    out, grad = weighted_sums(back_ref, mats_ref)
    out_ref[...] = (out + share_ref[:tok_rows].astype(jnp.float32)).astype(jnp.bfloat16)
    grad_ref[...] = (grad + share_ref[tok_rows:].astype(jnp.float32)).astype(jnp.bfloat16)


def combine(back, mats, other_share):
    half, double, width = back.shape
    tok_rows = mats.shape[2]
    shape = jax.ShapeDtypeStruct((tok_rows, width), jnp.bfloat16)
    block = width // 2
    out_spec = pl.BlockSpec((tok_rows, block), lambda i: (0, i))
    return pl.pallas_call(
        combine_kernel,
        grid=(2,),
        in_specs=[
            pl.BlockSpec((half, double, block), lambda i: (0, 0, i)),
            pl.BlockSpec(mats.shape, lambda i: (0, 0, 0)),
            pl.BlockSpec((2 * tok_rows, block), lambda i: (0, i)),
        ],
        out_specs=(out_spec, out_spec),
        out_shape=(shape, shape),
        compiler_params=PARAMS,
        cost_estimate=cost("combine"),
        name="combine",
    )(back, mats, other_share)


def adam_update(weights, first_moment, second_moment, gradient):
    first_new = BETA_ONE * first_moment + (1.0 - BETA_ONE) * gradient
    second_new = BETA_TWO * second_moment + (1.0 - BETA_TWO) * gradient * gradient
    adam_step = (
        LEARN_RATE
        * (first_new / (1.0 - BETA_ONE**STEP_COUNT))
        / (jnp.sqrt(second_new / (1.0 - BETA_TWO**STEP_COUNT)) + EPSILON)
    )
    weight_new = (weights.astype(jnp.float32) - adam_step).astype(jnp.bfloat16)
    return (weight_new, first_new, second_new)


def shards(
    tokens, gates, routes, cotangent, old_home, swap_flags, weights, first_moment, second_moment
):
    slot_count = lax.axis_size("ep")
    half = slot_count // 2
    own = lax.axis_index("ep")
    model_width = tokens.shape[1]
    is_swapped = jnp.sum(jnp.where(jnp.arange(half) == own % half, swap_flags, 0)) == 1
    groups = [
        [i for i in range(slot_count) if i // X_SIZE % 2 == z_half] for z_half in range(2)
    ]

    def exchange(rows):
        return lax.all_to_all(
            rows, "ep", split_axis=0, concat_axis=0, tiled=True, axis_index_groups=groups
        )

    home = old_home.reshape(1, -1)
    flags = swap_flags.reshape(1, -1)
    own_send, own_mats = route(routes.T, gates.T, home, flags, tokens, cotangent, "route_own")
    own_arrived = exchange(own_send)
    weights = jnp.where(is_swapped, partner(weights, half), weights)
    both = jnp.concatenate([tokens, cotangent], axis=0)
    pack = jnp.concatenate([routes.T.astype(jnp.float32), gates.T], axis=0)
    pack, both, _, _ = lax.optimization_barrier((pack, both, own_send, weights))
    pack, both = partner(pack, X_SIZE), partner(both, X_SIZE)
    top_count, tok_rows = routes.shape[1], tokens.shape[0]
    other_send, other_mats = route(
        pack[:top_count], pack[top_count:], home, flags, both[:tok_rows], both[tok_rows:], "route_other"
    )
    first_sent, second_sent = first_moment.astype(jnp.bfloat16), second_moment.astype(jnp.bfloat16)
    weights, _ = lax.optimization_barrier((weights, other_send))
    shards = gather_column(weights[0])
    other_send, own_arrived, first_sent, second_sent = lax.optimization_barrier(
        (other_send, own_arrived, first_sent, second_sent)
    )
    other_first = partner(first_sent, half)
    other_arrived = exchange(other_send)

    other_first, *shards = lax.optimization_barrier((other_first, *shards))
    gathered = gather_hidden(shards)
    own_back, own_act = expert(own_arrived, gathered, 2, "expert_own")
    other_arrived, own_back, own_act, second_sent = lax.optimization_barrier(
        (other_arrived, own_back, own_act, second_sent)
    )
    other_second = partner(second_sent, half)
    other_back, other_act = expert(other_arrived, gathered, 2, "expert_other")
    other_returned = exchange(other_back)
    other_act, other_second = lax.optimization_barrier((other_act, other_second))
    keep, give = gradient_terms(own_arrived, own_act, other_arrived, other_act)
    sums = core_sums(keep, give)
    own_back, other_returned, _ = lax.optimization_barrier((own_back, other_returned, sums[0]))
    own_returned = exchange(own_back)

    sums = [sums[0]] + [move_hidden(sums[dz], 2 * dz) for dz in range(1, len(sums))]
    other_mats, *sums = lax.optimization_barrier((other_mats, *sums))
    gradient = sum(part.astype(jnp.float32) for part in sums)[None]
    first_moment = jnp.where(is_swapped, other_first.astype(jnp.float32), first_moment)
    second_moment = jnp.where(is_swapped, other_second.astype(jnp.float32), second_moment)
    new_weights, new_first, new_second = adam_update(weights, first_moment, second_moment, gradient)

    other_share = partner(share(other_returned, other_mats), X_SIZE)
    layer_output_rows, token_gradient_rows = combine(own_returned, own_mats, other_share)
    return (layer_output_rows, token_gradient_rows, new_weights, new_first, new_second)


def solution(mesh):
    in_specs = (
        P(("ep", "tp"), None),
        P(("ep", "tp"), None),
        P(("ep", "tp"), None),
        P(("ep", "tp"), None),
        P(),
        P(),
        P("ep", None, "tp", None),
        P("ep", None, "tp", None),
        P("ep", None, "tp", None),
    )
    out_specs = (
        P(("ep", "tp"), None),
        P(("ep", "tp"), None),
        P("ep", None, "tp", None),
        P("ep", None, "tp", None),
        P("ep", None, "tp", None),
    )
    return jax.shard_map(shards, mesh=mesh, in_specs=in_specs, out_specs=out_specs, check_vma=False)
```

```python
import jax
import jax.numpy as jnp
from jax import lax
from jax.experimental import pallas as pl
from jax.experimental.pallas import tpu as pltpu
from jax.sharding import PartitionSpec as P

BETA_ONE = 0.9
BETA_TWO = 0.95
LEARN_RATE = 0.001
EPSILON = 1e-08
STEP_COUNT = 20.0

X_SIZE = 4
VMEM_LIMIT = 60 * 1024 * 1024
COST = {"route_own": 30, "route_other": 30, "expert_own": 27, "expert_other": 10, "terms": 30, "share": 36, "combine": 10, "assemble": 2, "pair": 2}
PARAMS = pltpu.CompilerParams(vmem_limit_bytes=VMEM_LIMIT)


def cost(name):
    return pl.CostEstimate(flops=COST[name] * 10**9, bytes_accessed=0, transcendentals=0)


def partner(array, apart):
    return lax.ppermute(array, "ep", [(i, i ^ apart) for i in range(lax.axis_size("ep"))])


def dot(a, b):
    return jnp.dot(a, b, preferred_element_type=jnp.float32)


def dot_last(a, b):
    return lax.dot_general(a, b, (((1,), (1,)), ((), ())), preferred_element_type=jnp.float32)


def dot_first(a, b):
    return lax.dot_general(a, b, (((0,), (0,)), ((), ())), preferred_element_type=jnp.float32)


def iota(shape, axis):
    return lax.broadcasted_iota(jnp.int32, shape, axis)


def route_kernel(routes_ref, gates_ref, home_ref, flags_ref, tokens_ref, cotangent_ref, send_ref, mats_ref):
    top_count, tok_rows = routes_ref.shape
    slot_count = home_ref.shape[1]
    pairs = slot_count // 2
    half, double, width = send_ref.shape
    capacity = double // 2
    rows = half * capacity
    z_half = lax.axis_index("ep") // X_SIZE % 2
    place = iota((half, 1), 0)
    slot = (place // X_SIZE * 2 + z_half) * X_SIZE + place % X_SIZE
    flag = jnp.sum(
        jnp.where(iota((half, pairs), 1) == slot % pairs, flags_ref[...].astype(jnp.float32), 0.0),
        axis=1,
        keepdims=True,
    )
    source = jnp.where(flag > 0, (slot + pairs) % slot_count, slot)
    expert = jnp.sum(
        jnp.where(iota((half, slot_count), 1) == source, home_ref[...].astype(jnp.float32), 0.0),
        axis=1,
        keepdims=True,
    )
    routes = routes_ref[...].astype(jnp.float32)
    named = jnp.zeros((half, tok_rows), jnp.float32)
    gate = jnp.zeros((half, tok_rows), jnp.float32)
    for k in range(top_count):
        hit = routes[k : k + 1, :] == expert
        named = named + jnp.where(hit, 1.0, 0.0)
        gate = gate + jnp.where(hit, gates_ref[k : k + 1, :], 0.0)
    earlier = iota((tok_rows, tok_rows), 0) < iota((tok_rows, tok_rows), 1)
    earlier = jnp.where(earlier, 1.0, 0.0).astype(jnp.bfloat16)
    rank = jnp.where(named > 0, dot(named.astype(jnp.bfloat16), earlier), -1.0)
    spread = iota((rows, half), 0) // capacity == iota((rows, half), 1)
    spread = jnp.where(spread, 1.0, 0.0).astype(jnp.bfloat16)
    gate_high = gate.astype(jnp.bfloat16)
    gate_low = (gate - gate_high.astype(jnp.float32)).astype(jnp.bfloat16)
    order = (iota((rows, 1), 0) % capacity).astype(jnp.float32)
    hit = dot(spread, rank.astype(jnp.bfloat16)) == order
    one = jnp.where(hit, 1.0, 0.0).astype(jnp.bfloat16)
    high = jnp.where(hit, dot(spread, gate_high), 0.0).astype(jnp.bfloat16)
    low = jnp.where(hit, dot(spread, gate_low), 0.0).astype(jnp.bfloat16)
    mats_ref[0] = high
    mats_ref[1] = low
    mats_ref[2] = one
    x_rows = dot(one, tokens_ref[...]).astype(jnp.bfloat16)
    send_ref[:, :capacity, :] = x_rows.reshape(half, capacity, width)
    cotangent = cotangent_ref[...]
    upstream = dot(
        jnp.concatenate([high, low], axis=1), jnp.concatenate([cotangent, cotangent], axis=0)
    ).astype(jnp.bfloat16)
    send_ref[:, capacity:, :] = upstream.reshape(half, capacity, width)


def route(routes, gates, home, flags, tokens, cotangent, name):
    top_count, tok_rows = routes.shape
    half = home.shape[1] // 2
    capacity = tok_rows * top_count // home.shape[1]
    return pl.pallas_call(
        route_kernel,
        out_shape=(
            jax.ShapeDtypeStruct((half, 2 * capacity, tokens.shape[1]), jnp.bfloat16),
            jax.ShapeDtypeStruct((3, half * capacity, tok_rows), jnp.bfloat16),
        ),
        compiler_params=PARAMS,
        cost_estimate=cost(name),
        name=name,
    )(routes, gates, home, flags, tokens, cotangent)


def expert_kernel(arrived_ref, weights_ref, back_ref, act_ref):
    sources, double, width = arrived_ref.shape
    capacity = double // 2
    hidden_width = weights_ref.shape[1]
    x_rows = arrived_ref[:, :capacity, :].reshape(sources * capacity, width)
    upstream = arrived_ref[:, capacity:, :].reshape(sources * capacity, width)
    inner = weights_ref[:2].reshape(2 * hidden_width, width)
    w_down = weights_ref[2]
    projected = dot_last(x_rows, inner)
    gate_pre = projected[:, :hidden_width]
    up_pre = projected[:, hidden_width:]
    sigmoid = jax.nn.sigmoid(gate_pre)
    hidden = (gate_pre * sigmoid * up_pre).astype(jnp.bfloat16)
    out = dot(hidden, w_down).astype(jnp.bfloat16)
    back_ref[:, :capacity, :] = out.reshape(sources, capacity, width)
    hidden_grad = dot_last(upstream, w_down)
    gate_grad = hidden_grad * up_pre * sigmoid * (1.0 + gate_pre * (1.0 - sigmoid))
    up_grad = hidden_grad * gate_pre * sigmoid
    act_ref[:, :hidden_width] = gate_grad.astype(jnp.bfloat16)
    act_ref[:, hidden_width : 2 * hidden_width] = up_grad.astype(jnp.bfloat16)
    act_ref[:, 2 * hidden_width :] = hidden
    row_grad = dot(act_ref[:, : 2 * hidden_width], inner).astype(jnp.bfloat16)
    back_ref[:, capacity:, :] = row_grad.reshape(sources, capacity, width)


def expert(arrived, weights, steps, name):
    sources, double, width = arrived.shape
    hidden_width = weights.shape[1]
    block = sources // steps
    rows = block * double // 2
    return pl.pallas_call(
        expert_kernel,
        grid=(steps,),
        in_specs=[
            pl.BlockSpec((block, double, width), lambda i: (i, 0, 0)),
            pl.BlockSpec((3, hidden_width, width), lambda i: (0, 0, 0)),
        ],
        out_specs=(
            pl.BlockSpec((block, double, width), lambda i: (i, 0, 0)),
            pl.BlockSpec((rows, 3 * hidden_width), lambda i: (i, 0)),
        ),
        out_shape=(
            jax.ShapeDtypeStruct(arrived.shape, jnp.bfloat16),
            jax.ShapeDtypeStruct((rows * steps, 3 * hidden_width), jnp.bfloat16),
        ),
        compiler_params=PARAMS,
        cost_estimate=cost(name),
        name=name,
    )(arrived, weights)


def terms_kernel(one_ref, one_act_ref, two_ref, two_act_ref, keep_ref, give_ref):
    sources, double, width = one_ref.shape
    capacity = double // 2
    matrices, half_width, _ = keep_ref.shape
    inner = (matrices - 1) * 2 * half_width

    def kind(ref, low):
        return ref[:, low : low + capacity, :].reshape(sources * capacity, width)

    def store(matrix, terms):
        keep_ref[matrix] = terms[:half_width]
        give_ref[matrix] = terms[half_width:]

    terms = (
        dot_first(one_act_ref[:, :inner], kind(one_ref, 0))
        + dot_first(two_act_ref[:, :inner], kind(two_ref, 0))
    ).astype(jnp.bfloat16)
    for matrix in range(matrices - 1):
        store(matrix, terms[matrix * 2 * half_width : (matrix + 1) * 2 * half_width])
    terms = (
        dot_first(one_act_ref[:, inner:], kind(one_ref, capacity))
        + dot_first(two_act_ref[:, inner:], kind(two_ref, capacity))
    ).astype(jnp.bfloat16)
    store(matrices - 1, terms)


def gradient_terms(one, one_act, two, two_act):
    shape = jax.ShapeDtypeStruct((3, one_act.shape[1] // 6, one.shape[2]), jnp.bfloat16)
    return pl.pallas_call(
        terms_kernel,
        out_shape=(shape, shape),
        compiler_params=PARAMS,
        cost_estimate=cost("terms"),
        name="terms",
    )(one, one_act, two, two_act)


def assemble_kernel(*refs):
    *shard_refs, other_ref, weights_ref = refs
    units = other_ref.shape[2]
    for place, ref in enumerate(shard_refs):
        weights_ref[:, place * units : (place + 1) * units, :] = ref[...]
    for dz in range(other_ref.shape[0]):
        place = len(shard_refs) + dz
        weights_ref[:, place * units : (place + 1) * units, :] = other_ref[dz]


def move_hidden(array, apart):
    return lax.ppermute(array, "tp", [(i, i ^ apart) for i in range(lax.axis_size("tp"))])


def gather_column(weights):
    return [weights] + [move_hidden(weights, 2 * dz) for dz in range(1, lax.axis_size("tp") // 2)]


def gather_hidden(shards):
    tp_count = lax.axis_size("tp")
    other = move_hidden(jnp.stack(shards), 1)
    matrices, units, width = shards[0].shape
    return pl.pallas_call(
        assemble_kernel,
        out_shape=jax.ShapeDtypeStruct((matrices, tp_count * units, width), jnp.bfloat16),
        compiler_params=PARAMS,
        cost_estimate=cost("assemble"),
        name="assemble",
    )(*shards, other)


def pair_kernel(keep_ref, given_ref, *sum_refs):
    units = sum_refs[0].shape[1]
    for dz, ref in enumerate(sum_refs):
        held = slice(dz * units, (dz + 1) * units)
        total = keep_ref[:, held, :].astype(jnp.float32) + given_ref[:, held, :].astype(jnp.float32)
        ref[...] = total.astype(jnp.bfloat16)


def core_sums(keep, give):
    given = move_hidden(give, 1)
    count = lax.axis_size("tp") // 2
    matrices, half_width, width = keep.shape
    shape = jax.ShapeDtypeStruct((matrices, half_width // count, width), jnp.bfloat16)
    return pl.pallas_call(
        pair_kernel,
        out_shape=[shape] * count,
        compiler_params=PARAMS,
        cost_estimate=cost("pair"),
        name="pair",
    )(keep, given)


def weighted_sums(back_ref, mats_ref):
    half, double, width = back_ref.shape
    capacity = double // 2
    out_rows = back_ref[:, :capacity, :].reshape(half * capacity, width)
    grad_rows = back_ref[:, capacity:, :].reshape(half * capacity, width)
    out = dot_first(mats_ref[0], out_rows) + dot_first(mats_ref[1], out_rows)
    return out, dot_first(mats_ref[2], grad_rows)


def share_kernel(back_ref, mats_ref, share_ref):
    tok_rows = mats_ref.shape[2]
    out, grad = weighted_sums(back_ref, mats_ref)
    share_ref[:tok_rows] = out.astype(jnp.bfloat16)
    share_ref[tok_rows:] = grad.astype(jnp.bfloat16)


def share(back, mats):
    return pl.pallas_call(
        share_kernel,
        out_shape=jax.ShapeDtypeStruct((2 * mats.shape[2], back.shape[2]), jnp.bfloat16),
        compiler_params=pltpu.CompilerParams(vmem_limit_bytes=24 * 1024 * 1024),
        cost_estimate=cost("share"),
        name="share",
    )(back, mats)


def combine_kernel(back_ref, mats_ref, share_ref, out_ref, grad_ref):
    tok_rows = mats_ref.shape[2]
    out, grad = weighted_sums(back_ref, mats_ref)
    out_ref[...] = (out + share_ref[:tok_rows].astype(jnp.float32)).astype(jnp.bfloat16)
    grad_ref[...] = (grad + share_ref[tok_rows:].astype(jnp.float32)).astype(jnp.bfloat16)


def combine(back, mats, other_share):
    half, double, width = back.shape
    tok_rows = mats.shape[2]
    shape = jax.ShapeDtypeStruct((tok_rows, width), jnp.bfloat16)
    block = width // 2
    out_spec = pl.BlockSpec((tok_rows, block), lambda i: (0, i))
    return pl.pallas_call(
        combine_kernel,
        grid=(2,),
        in_specs=[
            pl.BlockSpec((half, double, block), lambda i: (0, 0, i)),
            pl.BlockSpec(mats.shape, lambda i: (0, 0, 0)),
            pl.BlockSpec((2 * tok_rows, block), lambda i: (0, i)),
        ],
        out_specs=(out_spec, out_spec),
        out_shape=(shape, shape),
        compiler_params=PARAMS,
        cost_estimate=cost("combine"),
        name="combine",
    )(back, mats, other_share)


def adam_update(weights, first_moment, second_moment, gradient):
    first_new = BETA_ONE * first_moment + (1.0 - BETA_ONE) * gradient
    second_new = BETA_TWO * second_moment + (1.0 - BETA_TWO) * gradient * gradient
    adam_step = (
        LEARN_RATE
        * (first_new / (1.0 - BETA_ONE**STEP_COUNT))
        / (jnp.sqrt(second_new / (1.0 - BETA_TWO**STEP_COUNT)) + EPSILON)
    )
    weight_new = (weights.astype(jnp.float32) - adam_step).astype(jnp.bfloat16)
    return (weight_new, first_new, second_new)


def shards(
    tokens, gates, routes, cotangent, old_home, swap_flags, weights, first_moment, second_moment
):
    slot_count = lax.axis_size("ep")
    half = slot_count // 2
    own = lax.axis_index("ep")
    model_width = tokens.shape[1]
    is_swapped = jnp.sum(jnp.where(jnp.arange(half) == own % half, swap_flags, 0)) == 1
    groups = [
        [i for i in range(slot_count) if i // X_SIZE % 2 == z_half] for z_half in range(2)
    ]

    def exchange(rows):
        return lax.all_to_all(
            rows, "ep", split_axis=0, concat_axis=0, tiled=True, axis_index_groups=groups
        )

    home = old_home.reshape(1, -1)
    flags = swap_flags.reshape(1, -1)
    own_send, own_mats = route(routes.T, gates.T, home, flags, tokens, cotangent, "route_own")
    own_arrived = exchange(own_send)
    weights = jnp.where(is_swapped, partner(weights, half), weights)
    both = jnp.concatenate([tokens, cotangent], axis=0)
    pack = jnp.concatenate([routes.T.astype(jnp.float32), gates.T], axis=0)
    pack, both, _, _ = lax.optimization_barrier((pack, both, own_send, weights))
    pack, both = partner(pack, X_SIZE), partner(both, X_SIZE)
    top_count, tok_rows = routes.shape[1], tokens.shape[0]
    other_send, other_mats = route(
        pack[:top_count], pack[top_count:], home, flags, both[:tok_rows], both[tok_rows:], "route_other"
    )
    first_sent, second_sent = first_moment.astype(jnp.bfloat16), second_moment.astype(jnp.bfloat16)
    weights, _ = lax.optimization_barrier((weights, other_send))
    shards = gather_column(weights[0])
    other_send, own_arrived, first_sent, second_sent = lax.optimization_barrier(
        (other_send, own_arrived, first_sent, second_sent)
    )
    other_first = partner(first_sent, half)
    other_arrived = exchange(other_send)

    other_first, *shards = lax.optimization_barrier((other_first, *shards))
    gathered = gather_hidden(shards)
    own_back, own_act = expert(own_arrived, gathered, 2, "expert_own")
    other_arrived, own_back, own_act, second_sent = lax.optimization_barrier(
        (other_arrived, own_back, own_act, second_sent)
    )
    other_second = partner(second_sent, half)
    other_back, other_act = expert(other_arrived, gathered, 2, "expert_other")
    other_returned = exchange(other_back)
    other_act, other_second = lax.optimization_barrier((other_act, other_second))
    keep, give = gradient_terms(own_arrived, own_act, other_arrived, other_act)
    sums = core_sums(keep, give)
    own_back, other_returned, _ = lax.optimization_barrier((own_back, other_returned, sums[0]))
    own_returned = exchange(own_back)

    sums = [sums[0]] + [move_hidden(sums[dz], 2 * dz) for dz in range(1, len(sums))]
    other_mats, *sums = lax.optimization_barrier((other_mats, *sums))
    gradient = sum(part.astype(jnp.float32) for part in sums)[None]
    first_moment = jnp.where(is_swapped, other_first.astype(jnp.float32), first_moment)
    second_moment = jnp.where(is_swapped, other_second.astype(jnp.float32), second_moment)
    new_weights, new_first, new_second = adam_update(weights, first_moment, second_moment, gradient)

    other_share = partner(share(other_returned, other_mats), X_SIZE)
    layer_output_rows, token_gradient_rows = combine(own_returned, own_mats, other_share)
    return (layer_output_rows, token_gradient_rows, new_weights, new_first, new_second)


def solution(mesh):
    in_specs = (
        P(("ep", "tp"), None),
        P(("ep", "tp"), None),
        P(("ep", "tp"), None),
        P(("ep", "tp"), None),
        P(),
        P(),
        P("ep", None, "tp", None),
        P("ep", None, "tp", None),
        P("ep", None, "tp", None),
    )
    out_specs = (
        P(("ep", "tp"), None),
        P(("ep", "tp"), None),
        P("ep", None, "tp", None),
        P("ep", None, "tp", None),
        P("ep", None, "tp", None),
    )
    return jax.shard_map(shards, mesh=mesh, in_specs=in_specs, out_specs=out_specs, check_vma=False)
```

```python
import jax
import jax.numpy as jnp
from jax import lax
from jax.experimental import pallas as pl
from jax.experimental.pallas import tpu as pltpu
from jax.sharding import PartitionSpec as P

BETA_ONE = 0.9
BETA_TWO = 0.95
LEARN_RATE = 0.001
EPSILON = 1e-08
STEP_COUNT = 20.0

X_SIZE = 4
VMEM_LIMIT = 60 * 1024 * 1024
COST = {"route_own": 30, "route_other": 30, "expert_own": 27, "expert_other": 10, "terms": 30, "share": 36, "combine": 10, "assemble": 2, "pair": 2}
PARAMS = pltpu.CompilerParams(vmem_limit_bytes=VMEM_LIMIT)
SMALL = pltpu.CompilerParams(vmem_limit_bytes=24 * 1024 * 1024)


def cost(name):
    return pl.CostEstimate(flops=COST[name] * 10**9, bytes_accessed=0, transcendentals=0)


def partner(array, apart):
    return lax.ppermute(array, "ep", [(i, i ^ apart) for i in range(lax.axis_size("ep"))])


def dot(a, b):
    return jnp.dot(a, b, preferred_element_type=jnp.float32)


def dot_last(a, b):
    return lax.dot_general(a, b, (((1,), (1,)), ((), ())), preferred_element_type=jnp.float32)


def dot_first(a, b):
    return lax.dot_general(a, b, (((0,), (0,)), ((), ())), preferred_element_type=jnp.float32)


def iota(shape, axis):
    return lax.broadcasted_iota(jnp.int32, shape, axis)


def route_kernel(routes_ref, gates_ref, home_ref, flags_ref, tokens_ref, cotangent_ref, send_ref, mats_ref):
    top_count, tok_rows = routes_ref.shape
    slot_count = home_ref.shape[1]
    pairs = slot_count // 2
    half, double, width = send_ref.shape
    capacity = double // 2
    rows = half * capacity
    z_half = lax.axis_index("ep") // X_SIZE % 2
    place = iota((half, 1), 0)
    slot = (place // X_SIZE * 2 + z_half) * X_SIZE + place % X_SIZE
    flag = jnp.sum(
        jnp.where(iota((half, pairs), 1) == slot % pairs, flags_ref[...].astype(jnp.float32), 0.0),
        axis=1,
        keepdims=True,
    )
    source = jnp.where(flag > 0, (slot + pairs) % slot_count, slot)
    expert = jnp.sum(
        jnp.where(iota((half, slot_count), 1) == source, home_ref[...].astype(jnp.float32), 0.0),
        axis=1,
        keepdims=True,
    )
    routes = routes_ref[...].astype(jnp.float32)
    named = jnp.zeros((half, tok_rows), jnp.float32)
    gate = jnp.zeros((half, tok_rows), jnp.float32)
    for k in range(top_count):
        hit = routes[k : k + 1, :] == expert
        named = named + jnp.where(hit, 1.0, 0.0)
        gate = gate + jnp.where(hit, gates_ref[k : k + 1, :], 0.0)
    earlier = iota((tok_rows, tok_rows), 0) < iota((tok_rows, tok_rows), 1)
    earlier = jnp.where(earlier, 1.0, 0.0).astype(jnp.bfloat16)
    rank = jnp.where(named > 0, dot(named.astype(jnp.bfloat16), earlier), -1.0)
    spread = iota((rows, half), 0) // capacity == iota((rows, half), 1)
    spread = jnp.where(spread, 1.0, 0.0).astype(jnp.bfloat16)
    gate_high = gate.astype(jnp.bfloat16)
    gate_low = (gate - gate_high.astype(jnp.float32)).astype(jnp.bfloat16)
    order = (iota((rows, 1), 0) % capacity).astype(jnp.float32)
    hit = dot(spread, rank.astype(jnp.bfloat16)) == order
    one = jnp.where(hit, 1.0, 0.0).astype(jnp.bfloat16)
    high = jnp.where(hit, dot(spread, gate_high), 0.0).astype(jnp.bfloat16)
    low = jnp.where(hit, dot(spread, gate_low), 0.0).astype(jnp.bfloat16)
    mats_ref[0] = high
    mats_ref[1] = low
    mats_ref[2] = one
    x_rows = dot(one, tokens_ref[...]).astype(jnp.bfloat16)
    send_ref[:, :capacity, :] = x_rows.reshape(half, capacity, width)
    cotangent = cotangent_ref[...]
    upstream = dot(
        jnp.concatenate([high, low], axis=1), jnp.concatenate([cotangent, cotangent], axis=0)
    ).astype(jnp.bfloat16)
    send_ref[:, capacity:, :] = upstream.reshape(half, capacity, width)


def route(routes, gates, home, flags, tokens, cotangent, name):
    top_count, tok_rows = routes.shape
    half = home.shape[1] // 2
    capacity = tok_rows * top_count // home.shape[1]
    return pl.pallas_call(
        route_kernel,
        out_shape=(
            jax.ShapeDtypeStruct((half, 2 * capacity, tokens.shape[1]), jnp.bfloat16),
            jax.ShapeDtypeStruct((3, half * capacity, tok_rows), jnp.bfloat16),
        ),
        compiler_params=PARAMS,
        cost_estimate=cost(name),
        name=name,
    )(routes, gates, home, flags, tokens, cotangent)


def expert_kernel(arrived_ref, weights_ref, back_ref, act_ref):
    sources, double, width = arrived_ref.shape
    capacity = double // 2
    hidden_width = weights_ref.shape[1]
    x_rows = arrived_ref[:, :capacity, :].reshape(sources * capacity, width)
    upstream = arrived_ref[:, capacity:, :].reshape(sources * capacity, width)
    inner = weights_ref[:2].reshape(2 * hidden_width, width)
    w_down = weights_ref[2]
    projected = dot_last(x_rows, inner)
    gate_pre = projected[:, :hidden_width]
    up_pre = projected[:, hidden_width:]
    sigmoid = jax.nn.sigmoid(gate_pre)
    hidden = (gate_pre * sigmoid * up_pre).astype(jnp.bfloat16)
    out = dot(hidden, w_down).astype(jnp.bfloat16)
    back_ref[:, :capacity, :] = out.reshape(sources, capacity, width)
    hidden_grad = dot_last(upstream, w_down)
    gate_grad = hidden_grad * up_pre * sigmoid * (1.0 + gate_pre * (1.0 - sigmoid))
    up_grad = hidden_grad * gate_pre * sigmoid
    act_ref[:, :hidden_width] = gate_grad.astype(jnp.bfloat16)
    act_ref[:, hidden_width : 2 * hidden_width] = up_grad.astype(jnp.bfloat16)
    act_ref[:, 2 * hidden_width :] = hidden
    row_grad = dot(act_ref[:, : 2 * hidden_width], inner).astype(jnp.bfloat16)
    back_ref[:, capacity:, :] = row_grad.reshape(sources, capacity, width)


def expert(arrived, weights, steps, name):
    sources, double, width = arrived.shape
    hidden_width = weights.shape[1]
    block = sources // steps
    rows = block * double // 2
    return pl.pallas_call(
        expert_kernel,
        grid=(steps,),
        in_specs=[
            pl.BlockSpec((block, double, width), lambda i: (i, 0, 0)),
            pl.BlockSpec((3, hidden_width, width), lambda i: (0, 0, 0)),
        ],
        out_specs=(
            pl.BlockSpec((block, double, width), lambda i: (i, 0, 0)),
            pl.BlockSpec((rows, 3 * hidden_width), lambda i: (i, 0)),
        ),
        out_shape=(
            jax.ShapeDtypeStruct(arrived.shape, jnp.bfloat16),
            jax.ShapeDtypeStruct((rows * steps, 3 * hidden_width), jnp.bfloat16),
        ),
        compiler_params=PARAMS,
        cost_estimate=cost(name),
        name=name,
    )(arrived, weights)


def terms_kernel(one_ref, one_act_ref, two_ref, two_act_ref, keep_ref, give_ref):
    sources, double, width = one_ref.shape
    capacity = double // 2
    matrices, half_width, _ = keep_ref.shape
    inner = (matrices - 1) * 2 * half_width

    def kind(ref, low):
        return ref[:, low : low + capacity, :].reshape(sources * capacity, width)

    def store(matrix, terms):
        keep_ref[matrix] = terms[:half_width]
        give_ref[matrix] = terms[half_width:]

    terms = (
        dot_first(one_act_ref[:, :inner], kind(one_ref, 0))
        + dot_first(two_act_ref[:, :inner], kind(two_ref, 0))
    ).astype(jnp.bfloat16)
    for matrix in range(matrices - 1):
        store(matrix, terms[matrix * 2 * half_width : (matrix + 1) * 2 * half_width])
    terms = (
        dot_first(one_act_ref[:, inner:], kind(one_ref, capacity))
        + dot_first(two_act_ref[:, inner:], kind(two_ref, capacity))
    ).astype(jnp.bfloat16)
    store(matrices - 1, terms)


def gradient_terms(one, one_act, two, two_act):
    shape = jax.ShapeDtypeStruct((3, one_act.shape[1] // 6, one.shape[2]), jnp.bfloat16)
    return pl.pallas_call(
        terms_kernel,
        out_shape=(shape, shape),
        compiler_params=PARAMS,
        cost_estimate=cost("terms"),
        name="terms",
    )(one, one_act, two, two_act)


def assemble_kernel(*refs):
    *shard_refs, other_ref, weights_ref = refs
    units = other_ref.shape[2]
    for place, ref in enumerate(shard_refs):
        weights_ref[:, place * units : (place + 1) * units, :] = ref[...]
    for dz in range(other_ref.shape[0]):
        place = len(shard_refs) + dz
        weights_ref[:, place * units : (place + 1) * units, :] = other_ref[dz]


def move_hidden(array, apart):
    return lax.ppermute(array, "tp", [(i, i ^ apart) for i in range(lax.axis_size("tp"))])


def gather_column(weights):
    return [weights] + [move_hidden(weights, 2 * dz) for dz in range(1, lax.axis_size("tp") // 2)]


def gather_hidden(shards):
    tp_count = lax.axis_size("tp")
    other = move_hidden(jnp.stack(shards), 1)
    matrices, units, width = shards[0].shape
    return pl.pallas_call(
        assemble_kernel,
        out_shape=jax.ShapeDtypeStruct((matrices, tp_count * units, width), jnp.bfloat16),
        compiler_params=PARAMS,
        cost_estimate=cost("assemble"),
        name="assemble",
    )(*shards, other)


def pair_kernel(keep_ref, given_ref, *sum_refs):
    units = sum_refs[0].shape[1]
    for dz, ref in enumerate(sum_refs):
        held = slice(dz * units, (dz + 1) * units)
        total = keep_ref[:, held, :].astype(jnp.float32) + given_ref[:, held, :].astype(jnp.float32)
        ref[...] = total.astype(jnp.bfloat16)


def core_sums(keep, give):
    given = move_hidden(give, 1)
    count = lax.axis_size("tp") // 2
    matrices, half_width, width = keep.shape
    shape = jax.ShapeDtypeStruct((matrices, half_width // count, width), jnp.bfloat16)
    return pl.pallas_call(
        pair_kernel,
        out_shape=[shape] * count,
        compiler_params=PARAMS,
        cost_estimate=cost("pair"),
        name="pair",
    )(keep, given)


def weighted_sums(back_ref, mats_ref):
    half, double, width = back_ref.shape
    capacity = double // 2
    out_rows = back_ref[:, :capacity, :].reshape(half * capacity, width)
    grad_rows = back_ref[:, capacity:, :].reshape(half * capacity, width)
    out = dot(mats_ref[0], out_rows) + dot(mats_ref[1], out_rows)
    return out, dot(mats_ref[2], grad_rows)


def share_kernel(back_ref, mats_ref, share_ref):
    tok_rows = mats_ref.shape[1]
    out, grad = weighted_sums(back_ref, mats_ref)
    share_ref[:tok_rows] = out.astype(jnp.bfloat16)
    share_ref[tok_rows:] = grad.astype(jnp.bfloat16)


def share(back, mats):
    return pl.pallas_call(
        share_kernel,
        out_shape=jax.ShapeDtypeStruct((2 * mats.shape[1], back.shape[2]), jnp.bfloat16),
        compiler_params=SMALL,
        cost_estimate=cost("share"),
        name="share",
    )(back, mats)


def combine_kernel(back_ref, mats_ref, share_ref, out_ref, grad_ref):
    tok_rows = mats_ref.shape[1]
    out, grad = weighted_sums(back_ref, mats_ref)
    out_ref[...] = (out + share_ref[:tok_rows].astype(jnp.float32)).astype(jnp.bfloat16)
    grad_ref[...] = (grad + share_ref[tok_rows:].astype(jnp.float32)).astype(jnp.bfloat16)


def combine(back, mats, other_share):
    shape = jax.ShapeDtypeStruct((mats.shape[1], back.shape[2]), jnp.bfloat16)
    return pl.pallas_call(
        combine_kernel,
        out_shape=(shape, shape),
        compiler_params=SMALL,
        cost_estimate=cost("combine"),
        name="combine",
    )(back, mats, other_share)


def adam_update(weights, first_moment, second_moment, gradient):
    first_new = BETA_ONE * first_moment + (1.0 - BETA_ONE) * gradient
    second_new = BETA_TWO * second_moment + (1.0 - BETA_TWO) * gradient * gradient
    adam_step = (
        LEARN_RATE
        * (first_new / (1.0 - BETA_ONE**STEP_COUNT))
        / (jnp.sqrt(second_new / (1.0 - BETA_TWO**STEP_COUNT)) + EPSILON)
    )
    weight_new = (weights.astype(jnp.float32) - adam_step).astype(jnp.bfloat16)
    return (weight_new, first_new, second_new)


def shards(
    tokens, gates, routes, cotangent, old_home, swap_flags, weights, first_moment, second_moment
):
    slot_count = lax.axis_size("ep")
    half = slot_count // 2
    own = lax.axis_index("ep")
    model_width = tokens.shape[1]
    is_swapped = jnp.sum(jnp.where(jnp.arange(half) == own % half, swap_flags, 0)) == 1
    groups = [
        [i for i in range(slot_count) if i // X_SIZE % 2 == z_half] for z_half in range(2)
    ]

    def exchange(rows):
        return lax.all_to_all(
            rows, "ep", split_axis=0, concat_axis=0, tiled=True, axis_index_groups=groups
        )

    home = old_home.reshape(1, -1)
    flags = swap_flags.reshape(1, -1)
    own_send, own_mats = route(routes.T, gates.T, home, flags, tokens, cotangent, "route_own")
    own_arrived = exchange(own_send)
    weights = jnp.where(is_swapped, partner(weights, half), weights)
    both = jnp.concatenate([tokens, cotangent], axis=0)
    pack = jnp.concatenate([routes.T.astype(jnp.float32), gates.T], axis=0)
    pack, both, _, _ = lax.optimization_barrier((pack, both, own_send, weights))
    pack, both = partner(pack, X_SIZE), partner(both, X_SIZE)
    top_count, tok_rows = routes.shape[1], tokens.shape[0]
    other_send, other_mats = route(
        pack[:top_count], pack[top_count:], home, flags, both[:tok_rows], both[tok_rows:], "route_other"
    )
    first_sent, second_sent = first_moment.astype(jnp.bfloat16), second_moment.astype(jnp.bfloat16)
    weights, _ = lax.optimization_barrier((weights, other_send))
    shards = gather_column(weights[0])
    other_send, own_arrived, first_sent, second_sent = lax.optimization_barrier(
        (other_send, own_arrived, first_sent, second_sent)
    )
    other_first = partner(first_sent, half)
    other_arrived = exchange(other_send)

    other_first, *shards = lax.optimization_barrier((other_first, *shards))
    gathered = gather_hidden(shards)
    own_back, own_act = expert(own_arrived, gathered, 2, "expert_own")
    other_arrived, own_back, own_act, second_sent = lax.optimization_barrier(
        (other_arrived, own_back, own_act, second_sent)
    )
    other_second = partner(second_sent, half)
    other_back, other_act = expert(other_arrived, gathered, 2, "expert_other")
    other_returned = exchange(other_back)
    other_act, other_second = lax.optimization_barrier((other_act, other_second))
    keep, give = gradient_terms(own_arrived, own_act, other_arrived, other_act)
    sums = core_sums(keep, give)
    own_back, other_returned, _ = lax.optimization_barrier((own_back, other_returned, sums[0]))
    own_returned = exchange(own_back)

    sums = [sums[0]] + [move_hidden(sums[dz], 2 * dz) for dz in range(1, len(sums))]
    other_mats, *sums = lax.optimization_barrier((jnp.swapaxes(other_mats, 1, 2), *sums))
    gradient = sum(part.astype(jnp.float32) for part in sums)[None]
    first_moment = jnp.where(is_swapped, other_first.astype(jnp.float32), first_moment)
    second_moment = jnp.where(is_swapped, other_second.astype(jnp.float32), second_moment)
    new_weights, new_first, new_second = adam_update(weights, first_moment, second_moment, gradient)

    other_share = partner(share(other_returned, other_mats), X_SIZE)
    layer_output_rows, token_gradient_rows = combine(
        own_returned, jnp.swapaxes(own_mats, 1, 2), other_share
    )
    return (layer_output_rows, token_gradient_rows, new_weights, new_first, new_second)


def solution(mesh):
    in_specs = (
        P(("ep", "tp"), None),
        P(("ep", "tp"), None),
        P(("ep", "tp"), None),
        P(("ep", "tp"), None),
        P(),
        P(),
        P("ep", None, "tp", None),
        P("ep", None, "tp", None),
        P("ep", None, "tp", None),
    )
    out_specs = (
        P(("ep", "tp"), None),
        P(("ep", "tp"), None),
        P("ep", None, "tp", None),
        P("ep", None, "tp", None),
        P("ep", None, "tp", None),
    )
    return jax.shard_map(shards, mesh=mesh, in_specs=in_specs, out_specs=out_specs, check_vma=False)
```
